32 devices in a mesh: rep: 8 (over z, x), fsdp: 4 (over y, core).
Axes of the slice: x: 2, y: 2, z: 4, core: 2. Of those that a mesh axis runs over, the one named last changes fastest.
Arguments:
- tokens: bfloat16 [32768, 768], P(('rep', 'fsdp')), may hold values from -6 to 6
- cotangent: bfloat16 [32768, 768], P(('rep', 'fsdp')), may hold values from -6 to 6
- lengths: int32 [32, 4], P(('rep', 'fsdp')), may hold values from 0 to 1024, as said below
- w_qkv: float32 [768, 2304], P('fsdp'), may hold values from -0.21875 to 0.21875
- m_qkv: float32 [768, 2304], P('fsdp'), may hold values from -192 to 192
- v_qkv: float32 [768, 2304], P('fsdp'), may hold values from 4915.2 to 19660.8
- w_proj: float32 [768, 768], P('fsdp'), may hold values from -2 to 2
- m_proj: float32 [768, 768], P('fsdp'), may hold values from -20 to 20
- v_proj: float32 [768, 768], P('fsdp'), may hold values from 48 to 192
- w_ffn: float32 [768, 4096], P('fsdp'), may hold values from -0.21875 to 0.21875
- m_ffn: float32 [768, 4096], P('fsdp'), may hold values from -112 to 112
- v_ffn: float32 [768, 4096], P('fsdp'), may hold values from 1507.328 to 5898.24
- w_down: float32 [2048, 768], P('fsdp'), may hold values from -0.25 to 0.25
- m_down: float32 [2048, 768], P('fsdp'), may hold values from -56 to 56
- v_down: float32 [2048, 768], P('fsdp'), may hold values from 360.448 to 1507.328
- gains: float32 [2, 768], P(None, 'fsdp'), may hold values from 0.5 to 1.5
- m_gains: float32 [2, 768], P(None, 'fsdp'), may hold values from -320 to 320
- v_gains: float32 [2, 768], P(None, 'fsdp'), may hold values from 11468.8 to 45875.2
Outputs:
- block_out: bfloat16 [32768, 768], P(('rep', 'fsdp'))
- input_grad: float32 [32768, 768], P(('rep', 'fsdp'))
- qkv_moment: float32 [768, 2304], P('fsdp')
- qkv_second: float32 [768, 2304], P('fsdp')
- qkv_weight: float32 [768, 2304], P('fsdp')
- proj_moment: float32 [768, 768], P('fsdp')
- proj_second: float32 [768, 768], P('fsdp')
- proj_weight: float32 [768, 768], P('fsdp')
- ffn_moment: float32 [768, 4096], P('fsdp')
- ffn_second: float32 [768, 4096], P('fsdp')
- ffn_weight: float32 [768, 4096], P('fsdp')
- down_moment: float32 [2048, 768], P('fsdp')
- down_second: float32 [2048, 768], P('fsdp')
- down_weight: float32 [2048, 768], P('fsdp')
- gain_moment: float32 [2, 768], P(None, 'fsdp')
- gain_second: float32 [2, 768], P(None, 'fsdp')
- gain_weight: float32 [2, 768], P(None, 'fsdp')
The draws below stay inside these ranges and needn't reach their ends.
Inputs may be any that keep to these rules, and one draw needn't show every extreme that they name: A buffer's sequences lie end to end from its first row, and its lengths sum to at most 1024; rows after them are padding. Zero lengths may occur. In every draw one buffer holds a single sequence of 1024 tokens.
All inputs are finite; a program needn't handle non-finite values.
Results may differ from the reference program's by a relative error of at most 0.022.
Values may be sent and summed in bfloat16 or wider, within the bound.
A program may use at most 320 MiB of HBM per device.

```python
import math
import jax
import jax.numpy as jnp
from jax import lax

D = 768
HEADS = 12
HEAD_DIM = 64
FF = 2048
TOKCAP = 1024
SLOTS = 4
STEP = 10
QBLK = 512
TOKENS = 32768
N_REP = 8
N_FSDP = 4


def draw_lengths(key, part):
    key = jax.random.fold_in(key, 11)
    draw_key, pick_key = jax.random.split(key)
    shortest = TOKCAP // 16
    longest = TOKCAP // 4 + 1
    device_count = N_REP * N_FSDP
    spread = jax.random.randint(draw_key, (device_count, SLOTS), shortest, longest, dtype=jnp.int32)
    chosen = jax.random.randint(pick_key, (), 0, device_count, dtype=jnp.int32)
    single = jnp.where(jnp.arange(SLOTS, dtype=jnp.int32) == 0, TOKCAP, 0).astype(jnp.int32)
    picked = jnp.arange(device_count, dtype=jnp.int32) == chosen
    return jnp.where(picked[:, None], single[None, :], spread).astype(jnp.int32)


def steps_of(rng, shape, cuts, smallest, top_value):
    def one(position, parts):
        heights = jax.random.uniform(jax.random.fold_in(jax.random.fold_in(rng, 6), position), (parts,), jnp.float32, smallest / len(cuts), top_value / len(cuts))
        return jnp.repeat(jnp.exp(heights), shape[position] // parts).reshape((-1,) + (1,) * (len(shape) - position - 1))

    level = one(*cuts[0])
    for cut in cuts[1:]:
        level = level * one(*cut)
    return level


def noise(key, shape, scale, reach, cuts=(), kind=jnp.bfloat16):
    result = scale * jax.random.normal(key, shape, jnp.float32)
    if cuts:
        result = result * steps_of(key, shape, cuts, -0.22, 0.18)
    return jnp.clip(result, -reach, reach).astype(kind)


def setup_inputs(seed: int = 0) -> dict:
    key_list = jax.random.split(jax.random.key(seed), 19)
    tokens = noise(key_list[0], (TOKENS, D), 1.0, 6.0, ((0, 32),))
    cotangent = noise(key_list[1], (TOKENS, D), 1.0, 6.0, ((0, 32),))
    lengths = draw_lengths(jax.random.fold_in(key_list[18], 71), 0)
    w_qkv = noise(key_list[3], (D, 3 * D), D ** -0.5, 0.21875, ((0, 4),), jnp.float32)
    m_qkv = noise(key_list[4], (D, 3 * D), (0.24 * (0.6 * TOKCAP * N_REP * N_FSDP) ** 0.5), 192.0, ((0, 4),), jnp.float32)
    v_qkv = jnp.clip(jnp.exp(math.log(19660.8) - 1.3862944 * jax.random.uniform(key_list[5], (D, 3 * D), jnp.float32) ** steps_of(key_list[5], (D, 3 * D), ((0, 4),), -0.2, 0.2)), 4915.2, 19660.8)
    w_proj = noise(key_list[6], (D, D), (max(1, D * 10 // TOKCAP)) ** -0.5, 2.0, ((0, 4),), jnp.float32)
    m_proj = noise(key_list[7], (D, D), (0.6 * (N_REP * N_FSDP) ** 0.5), 20.0, ((0, 4),), jnp.float32)
    v_proj = jnp.clip(jnp.exp(math.log(192.0) - 1.3862944 * jax.random.uniform(key_list[8], (D, D), jnp.float32) ** steps_of(key_list[8], (D, D), ((0, 4),), -0.2, 0.2)), 48.0, 192.0)
    w_ffn = noise(key_list[9], (D, 2 * FF), D ** -0.5, 0.21875, ((0, 4),), jnp.float32)
    m_ffn = noise(key_list[10], (D, 2 * FF), (0.13 * (0.6 * TOKCAP * N_REP * N_FSDP) ** 0.5), 112.0, ((0, 4),), jnp.float32)
    v_ffn = jnp.clip(jnp.exp(math.log(5898.24) - 1.3643155 * jax.random.uniform(key_list[11], (D, 2 * FF), jnp.float32) ** steps_of(key_list[11], (D, 2 * FF), ((0, 4),), -0.2, 0.2)), 1507.328, 5898.24)
    w_down = noise(key_list[12], (FF, D), (FF // 4) ** -0.5, 0.25, ((0, 4),), jnp.float32)
    m_down = noise(key_list[13], (FF, D), (0.066 * (0.6 * TOKCAP * N_REP * N_FSDP) ** 0.5), 56.0, ((0, 4),), jnp.float32)
    v_down = jnp.clip(jnp.exp(math.log(1507.328) - 1.4307461 * jax.random.uniform(key_list[14], (FF, D), jnp.float32) ** steps_of(key_list[14], (FF, D), ((0, 4),), -0.2, 0.2)), 360.448, 1507.328)
    gains = jnp.clip(1.0 + 0.1 * jax.random.normal(key_list[15], (2, D), jnp.float32), 0.5, 1.5)
    m_gains = noise(key_list[16], (2, D), (0.36 * (0.6 * TOKCAP * N_REP * N_FSDP) ** 0.5), 320.0, ((1, 4),), jnp.float32)
    v_gains = jnp.clip(jnp.exp(math.log(45875.2) - 1.3862944 * jax.random.uniform(key_list[17], (2, D), jnp.float32) ** steps_of(key_list[17], (2, D), ((1, 4),), -0.2, 0.2)), 11468.8, 45875.2)
    return dict(tokens=tokens, cotangent=cotangent, lengths=lengths, w_qkv=w_qkv, m_qkv=m_qkv, v_qkv=v_qkv, w_proj=w_proj, m_proj=m_proj, v_proj=v_proj, w_ffn=w_ffn, m_ffn=m_ffn, v_ffn=v_ffn, w_down=w_down, m_down=m_down, v_down=v_down, gains=gains, m_gains=m_gains, v_gains=v_gains)


@jax.custom_vjp
def low(v):
    return lax.optimization_barrier(v.astype(jnp.bfloat16)).astype(jnp.float32)

@jax.custom_vjp
def low_back(v):
    return v

def low_keep(v):
    return (low(v), None)

def low_pass(kept, grad):
    return (grad,)

def back_keep(v):
    return (v, None)

def back_low(kept, grad):
    return (low(grad),)
low.defvjp(low_keep, low_pass)
low_back.defvjp(back_keep, back_low)
HIGH = lax.Precision.HIGHEST
norm_eps = 1e-05
rope_base = 10000.0
beta_first = 0.9
beta_second = 0.95
adam_eps = 1e-08
decay_rate = 0.1
masked_score = -1e+30

def positions(lengths_row, count):
    seq_ends = jnp.cumsum(lengths_row, dtype=jnp.int32)
    token_index = jnp.arange(count, dtype=jnp.int32)
    passed = token_index[:, None] >= seq_ends[None, :]
    segment = lax.optimization_barrier(jnp.sum(passed.astype(jnp.int32), axis=1, dtype=jnp.int32))
    starts = lax.optimization_barrier(jnp.max(jnp.where(passed, seq_ends[None, :], 0), axis=1))
    return (segment, token_index - starts, token_index < seq_ends[-1])

def tables(place, head_dim):
    half_width = head_dim // 2
    frequency = rope_base ** (-2.0 * jnp.arange(half_width, dtype=jnp.float32) / head_dim)
    angles = place.astype(jnp.float32)[:, None] * frequency[None, :]
    return (jnp.cos(angles)[:, None, :], jnp.sin(angles)[:, None, :])

def rotate(block, cosine, sine):
    half_width = block.shape[-1] // 2
    first_half = block[..., :half_width]
    second_half = block[..., half_width:]
    return jnp.concatenate([first_half * cosine - second_half * sine, second_half * cosine + first_half * sine], axis=-1)

def rms_scale(value, gain):
    inverse = lax.rsqrt(lax.optimization_barrier(jnp.mean(value * value, axis=-1, keepdims=True)) + norm_eps)
    return value * inverse * gain

def span_layer(buffer_in, lengths_row, qkv_w, proj_w, ffn_w, down_w, gain_w):
    segment, place, valid = positions(lengths_row, TOKCAP)
    cosine, sine = tables(place, HEAD_DIM)
    first_norm = low(rms_scale(buffer_in, gain_w[0]))
    projected = low_back(jnp.dot(first_norm, qkv_w, precision=HIGH)).reshape(TOKCAP, 3, HEADS, HEAD_DIM)
    queries = low(rotate(projected[:, 0], cosine, sine))
    keys_all = low(rotate(projected[:, 1], cosine, sine))
    values_all = low(projected[:, 2])
    score_scale = HEAD_DIM ** (-0.5)
    token_index = jnp.arange(TOKCAP, dtype=jnp.int32)

    def one_block(block_index):
        first_row = block_index * QBLK
        query_rows = lax.dynamic_slice_in_dim(queries, first_row, QBLK, 0)
        row_segment = lax.dynamic_slice_in_dim(segment, first_row, QBLK, 0)
        row_index = first_row + jnp.arange(QBLK, dtype=jnp.int32)
        allowed = (row_segment[:, None] == segment[None, :]) & (token_index[None, :] <= row_index[:, None])
        raw_scores = low_back(jnp.einsum('qhd,khd->hqk', query_rows, keys_all, precision=HIGH))
        scores = jnp.where(allowed[None], raw_scores * score_scale, masked_score)
        largest = lax.optimization_barrier(jnp.max(scores, axis=-1, keepdims=True))
        summed = lax.optimization_barrier(jnp.sum(jnp.exp(scores - largest), axis=-1, keepdims=True))
        weights = low(jnp.exp(scores - (largest + jnp.log(summed))))
        return jnp.einsum('hqk,khd->qhd', weights, values_all, precision=HIGH)
    blocks = lax.map(jax.checkpoint(one_block), jnp.arange(TOKCAP // QBLK, dtype=jnp.int32))
    attended = low(low_back(blocks.reshape(TOKCAP, D)))
    middle = buffer_in + low_back(jnp.dot(attended, proj_w, precision=HIGH))
    second_norm = low(rms_scale(middle, gain_w[1]))
    gate_up = low_back(jnp.dot(second_norm, ffn_w, precision=HIGH))
    inner = low(jax.nn.silu(gate_up[:, :FF]) * gate_up[:, FF:])
    return middle + low_back(jnp.dot(inner, down_w, precision=HIGH))

def adamw(weight, first, second, grad, rate):
    first_new = beta_first * first + (1.0 - beta_first) * grad
    second_new = beta_second * second + (1.0 - beta_second) * grad * grad
    first_hat = first_new / (1.0 - beta_first ** STEP)
    second_hat = second_new / (1.0 - beta_second ** STEP)
    return (first_new, second_new, weight - rate * (first_hat / (jnp.sqrt(second_hat) + adam_eps) + decay_rate * weight))

def reference(tokens, cotangent, lengths, w_qkv, m_qkv, v_qkv, w_proj, m_proj, v_proj, w_ffn, m_ffn, v_ffn, w_down, m_down, v_down, gains, m_gains, v_gains):
    buffers = N_REP * N_FSDP
    inputs = tokens.astype(jnp.float32).reshape(buffers, TOKCAP, D)
    layer = jax.checkpoint(span_layer)

    def forward(values_in, qkv_w, proj_w, ffn_w, down_w, gain_w):
        qkv_low = low(qkv_w)
        proj_low = low(proj_w)
        ffn_low = low(ffn_w)
        down_low = low(down_w)
        gain_low = low(gain_w)

        def one_buffer(carry, item):
            buffer_in, lengths_row = item
            return (carry, layer(buffer_in, lengths_row, qkv_low, proj_low, ffn_low, down_low, gain_low))
        carry, outputs = lax.scan(one_buffer, jnp.zeros((), jnp.float32), (values_in, lengths))
        return outputs
    outputs, pullback = jax.vjp(forward, inputs, w_qkv, w_proj, w_ffn, w_down, gains)
    valid = jax.vmap(lambda row: positions(row, TOKCAP)[2])(lengths)
    incoming = cotangent.astype(jnp.float32).reshape(buffers, TOKCAP, D) * valid[:, :, None].astype(jnp.float32)
    grad_in, grad_qkv, grad_proj, grad_ffn, grad_down, grad_gain = pullback(incoming)
    rate_wide = 3.0 * D ** (-0.5)
    rate_proj = 3.0 * (TOKCAP / (10.0 * D)) ** 0.5
    rate_down = 6.0 * FF ** (-0.5)
    qkv_new = adamw(w_qkv, m_qkv, v_qkv, grad_qkv, rate_wide)
    proj_new = adamw(w_proj, m_proj, v_proj, grad_proj, rate_proj)
    ffn_new = adamw(w_ffn, m_ffn, v_ffn, grad_ffn, rate_wide)
    down_new = adamw(w_down, m_down, v_down, grad_down, rate_down)
    gain_new = adamw(gains, m_gains, v_gains, grad_gain, 1.0)
    block_out = outputs.reshape(TOKENS, D).astype(jnp.bfloat16)
    input_grad = grad_in.reshape(TOKENS, D)
    return (block_out, input_grad, qkv_new[0], qkv_new[1], qkv_new[2], proj_new[0], proj_new[1], proj_new[2], ffn_new[0], ffn_new[1], ffn_new[2], down_new[0], down_new[1], down_new[2], gain_new[0], gain_new[1], gain_new[2])
```

```python
import functools

import jax
import jax.numpy as jnp
from jax import lax
from jax.experimental import pallas as pl
from jax.experimental.pallas import tpu as pltpu
from jax.sharding import PartitionSpec as P

HEADS = 12
FF = 2048
STEP = 10
norm_eps = 1e-05
rope_base = 10000.0
beta_first = 0.9
beta_second = 0.95
adam_eps = 1e-08
decay_rate = 0.1
LOG2E = 1.4426950408889634
MASKED = -1e30
MESH = pl.DeviceIdType.MESH
f32 = jnp.float32
bf16 = jnp.bfloat16
BLK = 256
CHUNKS = 12
PIECE = 144
SLOTS = 9
ANY = pl.BlockSpec(memory_space=pl.ANY)
VM = pl.BlockSpec(memory_space=pltpu.VMEM)
SM = pl.BlockSpec(memory_space=pltpu.SMEM)


def dot(a, b, ca, cb):
    return lax.dot_general(a, b, (((ca,), (cb,)), ((), ())), preferred_element_type=f32)


def joined(ref, first, number):
    return jnp.concatenate([ref[first + i] for i in range(number)], axis=1)


def rows_of(i):
    return pl.ds(pl.multiple_of(i * BLK, BLK), BLK)


def lane_head(h, shape):
    return (lax.broadcasted_iota(jnp.int32, shape, 1) // 64) == h


def seq_ends(len_ref):
    total = 0
    ends = []
    for j in range(4):
        total = total + len_ref[0, j]
        ends.append(total)
    return ends


def fill_bias(ends, bias, count):
    q = lax.broadcasted_iota(jnp.int32, (1, count), 1)
    sq = sum((q >= e).astype(jnp.int32) for e in ends)

    @pl.loop(0, count // BLK)
    def _(j):
        k = lax.broadcasted_iota(jnp.int32, (BLK, 1), 0) + j * BLK
        sk = sum((k >= e).astype(jnp.int32) for e in ends)
        bias[rows_of(j), :] = jnp.where((sk == sq) & (k <= q), 0.0, MASKED)


def rope(block, cosine, sine, sign):
    lane = lax.broadcasted_iota(jnp.int32, block.shape, 1)
    swapped = jnp.where(lane % 64 < 32, pltpu.roll(block, 96, 1), pltpu.roll(block, 32, 1))
    if sign > 0:
        return block * cosine + swapped * sine
    return block * cosine - swapped * sine


def remote(src, dst, send_sem, recv_sem, device):
    return pltpu.make_async_remote_copy(
        src_ref=src, dst_ref=dst, send_sem=send_sem, recv_sem=recv_sem,
        device_id=device, device_id_type=MESH)


def unit_rows(value):
    inverse = lax.rsqrt(jnp.mean(value * value, axis=-1, keepdims=True) + norm_eps)
    return value * inverse, inverse


class Gather:
    def __init__(self, own, full, first, blocks, shard_rows, sems, index, ids):
        self.own, self.full, self.first, self.blocks, self.n = own, full, first, blocks, shard_rows
        self.ssem, self.rsem, self.w, self.ids = sems[0], sems[1], index, ids
        rep, fs = ids["rep"], ids["fsdp"]
        self.b0, self.b1 = rep % 2, (rep // 2) % 2
        self.q = rep % 4
        self.far = (fs + 2) % 4
        self.fs = fs
        self.quarter = shard_rows // 4

    def part(self, shard, quarter, quarters, half=None):
        row = pl.multiple_of(shard * self.n + quarter * self.quarter, 16)
        first, blocks = self.first, self.blocks
        if half is not None:
            blocks = blocks // 2
            first = first + half * blocks
        return self.full.at[pl.ds(first, blocks), pl.ds(row, quarters * self.quarter), :]

    def cp(self, i, ref, device, src=None):
        return remote(ref if src is None else src, ref, self.ssem.at[self.w, i], self.rsem.at[self.w, i], device)

    def copy(self, i):
        d = self.ids
        p, far, fs, q = self.part, self.far, self.fs, self.q
        q1 = (1 - self.b0) + 2 * self.b1
        q2 = self.b0 + 2 * (1 - self.b1)
        q3 = (1 - self.b0) + 2 * (1 - self.b1)
        own = own_quarter = None
        if self.own is not None:
            own = self.own.at[pl.ds(self.first, self.blocks)]
            own_quarter = self.own.at[pl.ds(self.first, self.blocks), pl.ds(pl.multiple_of(q * self.quarter, 16), self.quarter), :]
        return [
            lambda: self.cp(0, p(fs, 0, 4), d["core"], own),
            lambda: self.cp(1, p(fs, q, 1), d["y"], own_quarter),
            lambda: self.cp(2, p(far, q, 1, 0), d["bit0"]),
            lambda: self.cp(3, p(far, q, 1, 1), d["bit1"]),
            lambda: self.cp(4, p(far, q, 1), d["core"]),
            lambda: self.cp(5, p(far, 2 * self.b1, 2, 0), d["bit1"]),
            lambda: self.cp(6, p(far, q, 1, 1), d["bit0"]),
            lambda: self.cp(7, p(far, q2, 1, 1), d["bit0"]),
            lambda: self.cp(8, p(far, q1, 1, 0), d["core"]),
            lambda: self.cp(9, p(far, q2, 1, 1), d["core"]),
            lambda: self.cp(10, p(far, 2 * (1 - self.b1), 2, 0), d["core"]),
            lambda: self.cp(11, p(far, q1, 1, 1), d["core"]),
            lambda: self.cp(12, p(far, q3, 1, 1), d["core"]),
        ][i]()

    def step(self, waits, starts):
        for i in waits:
            self.copy(i).wait_recv()
        for i in starts:
            self.copy(i).start()

    def start(self):
        self.step((), (1, 0))

    def second(self):
        self.step((1,), (2, 3, 4))

    def third(self):
        self.step((2, 3), (5, 6, 7, 8, 9))

    def fourth(self):
        self.step((5, 6, 7), (10, 11, 12))

    def arrive(self):
        self.step((0, 4, 8, 9, 10, 11, 12), ())

    def sent(self):
        for i in range(13):
            self.copy(i).wait_send()


def partners(rep, fs, reps):
    found = {"rep": rep, "fsdp": fs, "core": (rep, fs ^ 1), "y": (rep, fs ^ 2)}
    for b in range(reps.bit_length() - 1):
        found["bit%d" % b] = (rep ^ (1 << b), fs)
    return found


def meet(ids, names):
    barrier = pltpu.get_barrier_semaphore()
    for name in names:
        pl.semaphore_signal(barrier, inc=1, device_id=ids[name], device_id_type=MESH)
    pl.semaphore_wait(barrier, len(names))


def place_gains(ref, rows, fs):
    ref[...] = pltpu.roll(ref[...], fs * rows, 1)


def forward_kernel(reps, len_ref, x_in, gain_in, freq_ref, wq_in, wo_in, wf_in, wd_in,
                   wq_out, wo_out, wf_out, wd_out, q_out, k_out, v_out, a_out, log_out, mid_out, gain_out, cos_out, sin_out,
                   wq_s, wo_s, st_q, st_o, st_f, st_d, own_f, own_d, gain_a, gain_b, gain_c, x_s, cos_s, sin_s,
                   h1_s, q_s, k_s, vt_s, v_s, a_s, log_s, mid_s, bias,
                   load_sem, store_sem, send_sem, recv_sem, gsend_sem, grecv_sem):
    count, width = x_s.shape
    pairs = width // 128
    rows = width // 4
    rep, fs = lax.axis_index("rep"), lax.axis_index("fsdp")
    ids = partners(rep, fs, reps)
    load_q = pltpu.make_async_copy(wq_in, st_q, load_sem.at[0])
    load_x = pltpu.make_async_copy(x_in, x_s, load_sem.at[1])
    load_o = pltpu.make_async_copy(wo_in, st_o, load_sem.at[2])
    load_f = pltpu.make_async_copy(wf_in, st_f, load_sem.at[3])
    load_d = pltpu.make_async_copy(wd_in, st_d, load_sem.at[4])
    for c in (load_q, load_x, load_o, load_f, load_d):
        c.start()
    gain_a[...] = jnp.zeros_like(gain_a)
    gain_a[0:2, 0:rows] = gain_in[...].astype(bf16).astype(f32)
    gain_a[...] = pltpu.roll(gain_a[...], fs * rows, 1)
    meet(ids, ("core", "y", "bit0", "bit1"))

    sems = (send_sem, recv_sem)
    near = [Gather(None, wq_s, 6 * c, 6, rows, sems, c, ids) for c in range(3)]
    proj = Gather(None, wo_s, 0, 6, rows, sems, 3, ids)
    wide = [Gather(own_f, wf_out, 8 * j, 8, rows, sems, 4 + j, ids) for j in range(4)]
    down = Gather(own_d, wd_out, 0, 4, FF // 16, sems, 8, ids)

    g_core = remote(gain_a, gain_b, gsend_sem.at[0], grecv_sem.at[0], ids["core"])
    g_core.start()
    own_rows = pl.ds(pl.multiple_of(fs * rows, 16), rows)
    load_q.wait()
    for c in range(3):
        for t in range(3):
            for i in range(2):
                col = t * width + (2 * c + i) * 128
                wq_s[6 * c + 2 * t + i, own_rows, :] = st_q[:, col:col + 128].astype(bf16)
        near[c].start()
    g_core.wait()
    gain_c[0] = gain_a[...] + gain_b[...]
    g_y = remote(gain_c.at[0], gain_c.at[1], gsend_sem.at[1], grecv_sem.at[1], ids["y"])
    g_y.start()
    load_o.wait()
    for i in range(6):
        wo_s[i, own_rows, :] = st_o[:, 128 * i:128 * i + 128].astype(bf16)
    load_f.wait()
    for j in range(4):
        for n in range(8):
            col = (4 * n + j) * 128
            own_f[8 * j + n] = st_f[:, col:col + 128].astype(bf16)
    near[0].second()
    load_d.wait()
    for j in range(4):
        own_d[j] = st_d[128 * j:128 * j + 128, :].astype(bf16)
    near[1].second()
    near[2].second()
    proj.start()
    wide[0].start()
    stores = [
        pltpu.make_async_copy(own_f, wf_out.at[:, own_rows, :], store_sem.at[0]),
        pltpu.make_async_copy(own_d, wd_out.at[:, pl.ds(pl.multiple_of(fs * (FF // 16), 16), FF // 16), :], store_sem.at[1]),
    ]
    for c in stores:
        c.start()
    near[0].third()
    ends = seq_ends(len_ref)
    token = lax.broadcasted_iota(jnp.int32, (1, count), 1)
    start = jnp.zeros((1, count), jnp.int32)
    for e in ends:
        start = jnp.where(token >= e, e, start)
    angle = freq_ref[:, 0:1] * (token - start).astype(f32)
    cosine, sine = jnp.cos(angle), jnp.sin(angle)
    cos_s[...] = jnp.concatenate([cosine] * 4, axis=0).T
    sin_s[...] = jnp.concatenate([-sine, sine, -sine, sine], axis=0).T
    near[1].third()
    near[2].third()
    g_y.wait()
    gain_out[...] = gain_c[0] + gain_c[1]
    g1 = gain_out[0:1, :]
    load_x.wait()

    @pl.loop(0, count // BLK)
    def _(i):
        blk = pl.ds(pl.multiple_of(i * BLK, BLK), BLK)
        x = x_s[blk, :].astype(f32)
        inverse = lax.rsqrt(jnp.mean(x * x, axis=-1, keepdims=True) + norm_eps)
        h1_s[blk, :] = (x * inverse * g1).astype(bf16)

    near[0].fourth()
    near[1].fourth()
    wide[1].start()
    near[2].fourth()
    wide[2].start()
    fill_bias(ends, bias, count)
    proj.second()

    def project(c):
        h1 = h1_s[...]
        for t in range(3):
            block = dot(h1, joined(wq_s, 6 * c + 2 * t, 2), 1, 0)
            for i in range(2):
                p = 2 * c + i
                piece = block[:, 128 * i:128 * i + 128]
                if t == 0:
                    q_s[p] = (rope(piece, cos_s[...], sin_s[...], 1) * (LOG2E / 8)).astype(bf16)
                elif t == 1:
                    k_s[p] = rope(piece, cos_s[...], sin_s[...], 1).astype(bf16)
                else:
                    v_s[p] = piece.astype(bf16)
                    vt_s[p] = piece.T.astype(bf16)

    def scores(p, i, h):
        q = q_s[p, i * BLK:(i + 1) * BLK, :]
        return dot(k_s[p, :BLK * (i + 1), :], jnp.where(lane_head(h, q.shape), q, 0), 1, 1)

    def soft(p, i, h, s):
        s = s + bias[:BLK * (i + 1), i * BLK:(i + 1) * BLK]
        largest = jnp.max(s, axis=0, keepdims=True)
        e = jnp.exp2(s - largest)
        total = jnp.sum(e, axis=0, keepdims=True)
        log_s[p, h:h + 1, i * BLK:(i + 1) * BLK] = largest + jnp.log2(total)
        return e.astype(bf16), total

    def mix(p, i, h, e, total):
        return dot(vt_s[p, 64 * h:64 * h + 64, :BLK * (i + 1)], e, 1, 0) * (1.0 / total)

    def attend(p):
        tasks = [(i, h) for i in range(count // BLK) for h in range(2)]
        s = scores(p, *tasks[0])
        held = None
        outs = {}
        for n, task in enumerate(tasks):
            ahead = scores(p, *tasks[n + 1]) if n + 1 < len(tasks) else None
            weighted = soft(p, *task, s)
            if held is not None:
                outs[held[0]] = mix(p, *held[0], *held[1])
            held = (task, weighted)
            s = ahead
        outs[held[0]] = mix(p, *held[0], *held[1])
        cols = pl.ds(pl.multiple_of(p * 128, 128), 128)
        for i in range(count // BLK):
            a_s[i * BLK:(i + 1) * BLK, cols] = jnp.concatenate([outs[i, 0], outs[i, 1]], axis=0).T.astype(bf16)

    before = [
        [near[0].arrive],
        [wide[1].second, wide[0].third, near[1].arrive],
        [wide[2].third, wide[1].fourth, wide[3].second, near[2].arrive],
    ]
    between = [
        [wide[0].second, wide[3].start, down.start, proj.third],
        [wide[1].third, wide[2].second, wide[0].fourth, proj.fourth],
        [wide[3].third, down.second, wide[2].fourth],
    ]
    last = [down.third, wide[3].fourth]

    for c in range(3):
        for step in before[c]:
            step()
        project(c)
        for step in between[c]:
            step()

        @pl.loop(2 * c, 2 * c + 2)
        def _(p):
            attend(p)
    for step in last:
        step()
    for i, (src, dst) in enumerate(((wq_s, wq_out), (q_s, q_out), (k_s, k_out), (v_s, v_out), (cos_s, cos_out), (sin_s, sin_out))):
        c = pltpu.make_async_copy(src, dst, store_sem.at[3 + i])
        c.start()
        stores.append(c)
    proj.arrive()
    for i, (src, dst) in enumerate(((wo_s, wo_out), (a_s, a_out), (log_s, log_out))):
        c = pltpu.make_async_copy(src, dst, store_sem.at[9 + i])
        c.start()
        stores.append(c)

    @pl.loop(0, count // BLK)
    def _(i):
        blk = pl.ds(pl.multiple_of(i * BLK, BLK), BLK)
        mid_s[blk, :] = x_s[blk, :].astype(f32) + dot(a_s[blk, :], joined(wo_s, 0, 6), 1, 0)
    c = pltpu.make_async_copy(mid_s, mid_out, store_sem.at[12])
    c.start()
    stores.append(c)
    down.fourth()
    for g in wide + [down]:
        g.arrive()
    for g in near + [proj] + wide + [down]:
        g.sent()
    for c in stores:
        c.wait()


def frequencies():
    half = 32
    frequency = rope_base ** (-2.0 * jnp.arange(half, dtype=f32) / (2 * half))
    return jnp.broadcast_to(frequency[:, None], (half, 128))


def forward(reps, lengths, tokens, gains, w_qkv, w_proj, w_ffn, w_down):
    count, width = tokens.shape
    pairs = width // 128
    S = jax.ShapeDtypeStruct
    V = pltpu.VMEM
    rows = width // 4
    dma = pltpu.SemaphoreType.DMA
    return pl.pallas_call(
        functools.partial(forward_kernel, reps),
        name="gather_forward",
        in_specs=[SM, ANY, VM, VM, ANY, ANY, ANY, ANY],
        out_specs=[ANY] * 10 + [VM] + [ANY] * 2,
        out_shape=[S((18, width, 128), bf16), S((6, width, 128), bf16), S((32, width, 128), bf16), S((4, FF // 4, width), bf16),
                   S((pairs, count, 128), bf16), S((pairs, count, 128), bf16), S((pairs, count, 128), bf16),
                   S((count, width), bf16), S((pairs, 8, count), f32), S((count, width), f32), S((8, width), f32),
                   S((count, 128), f32), S((count, 128), f32)],
        scratch_shapes=[
            V((18, width, 128), bf16), V((6, width, 128), bf16), V((rows, 3 * width), f32), V((rows, width), f32),
            V((rows, 2 * FF), f32), V((FF // 4, width), f32), V((32, rows, 128), bf16), V((4, FF // 16, width), bf16),
            V((8, width), f32), V((8, width), f32), V((2, 8, width), f32),
            V((count, width), bf16), V((count, 128), f32), V((count, 128), f32),
            V((count, width), bf16), V((pairs, count, 128), bf16), V((pairs, count, 128), bf16),
            V((pairs, 128, count), bf16), V((pairs, count, 128), bf16), V((count, width), bf16),
            V((pairs, 8, count), f32), V((count, width), f32), V((count, count), f32),
            dma((5,)), dma((13,)), dma((9, 13)), dma((9, 13)), dma((2,)), dma((2,))],
        compiler_params=pltpu.CompilerParams(collective_id=0, has_side_effects=True, vmem_limit_bytes=60 * 2**20),
    )(lengths, tokens, gains, frequencies(), w_qkv, w_proj, w_ffn, w_down)


class Reduce:
    def __init__(self, ids, reps, grad, slots, kept, out, sems, out_sem):
        self.ids = ids
        self.grad, self.slots, self.kept, self.out = grad, slots, kept, out
        self.ssem, self.rsem = sems
        self.out_sem = out_sem
        rep, fs = ids["rep"], ids["fsdp"]
        self.core, self.y = fs % 2, fs // 2
        self.b = [rep // (1 << i) % 2 for i in range(3)]
        self.base = [4 * self.b[0], 4 * self.b[0] + 2 * self.b[1], 4 * self.b[0] + 2 * self.b[1] + self.b[2]]
        self.extra = reps.bit_length() - 1 - 3
        self.stages = 9 + self.extra
        self.at = [0] * CHUNKS
        self.ready = 0

    def cp(self, kind, n, src, dst, device):
        return remote(src, dst, self.ssem.at[kind, n % 2], self.rsem.at[kind, n % 2], self.ids[device])

    def exchange(self, k, n):
        g = self.grad.at[n % SLOTS]
        mine = g.at[self.core, self.y]
        keep = self.kept.at[n]
        b, base = self.b, self.base
        par = n % 2
        if k == 0:
            return self.cp(0, n, g.at[1 - self.core], self.slots[0].at[par], "core")
        if k == 1:
            return self.cp(1, n, g.at[self.core, 1 - self.y], self.slots[1].at[par], "y")
        if k == 2:
            return self.cp(2, n, mine.at[pl.ds(4 * (1 - b[0]), 4)], self.slots[2].at[par], "bit0")
        if k == 3:
            return self.cp(3, n, mine.at[pl.ds(base[0] + 2 * (1 - b[1]), 2)], self.slots[3].at[par], "bit1")
        if k == 4:
            return self.cp(4, n, mine.at[pl.ds(base[1] + 1 - b[2], 1)], self.slots[4].at[par], "bit2")
        if k < 5 + self.extra:
            return self.cp(k, n, keep.at[pl.ds(base[2], 1)], self.slots[k].at[par], "bit%d" % (k - 2))
        k -= self.extra
        width = (1, 2, 4)[k - 5]
        part = keep.at[pl.ds(base[7 - k], width)]
        return self.cp(k + self.extra, n, part, part, "bit%d" % (7 - k))

    def add(self, n, first, number, slot, offset, target=None):
        mine = self.grad.at[n % SLOTS, self.core, self.y]

        @pl.loop(0, number)
        def _(i):
            total = mine[first + i].astype(f32) + slot[offset + i].astype(f32)
            (mine if target is None else target)[first + i] = total.astype(bf16)

    def stage(self, k, n):
        par = n % 2
        b, base = self.b, self.base
        if k > 0:
            if k < self.stages:
                self.exchange(k - 1, n).wait()
        if k == 0:
            self.exchange(0, n).start()
        elif k == 1:
            g, slot = self.grad.at[n % SLOTS, self.core], self.slots[0].at[par]
            for y in (1 - self.y, self.y):
                @pl.loop(0, 8)
                def _(i):
                    g[y, i] = (g[y, i].astype(f32) + slot[y, i].astype(f32)).astype(bf16)
                if y is not self.y:
                    self.exchange(1, n).start()
        elif k == 2:
            self.add(n, 4 * (1 - b[0]), 4, self.slots[1].at[par], 4 * (1 - b[0]))
            self.exchange(2, n).start()
            self.add(n, base[0], 4, self.slots[1].at[par], base[0])
        elif k == 3:
            other = 2 * (1 - b[1])
            self.add(n, base[0] + other, 2, self.slots[2].at[par], other)
            self.exchange(3, n).start()
            self.add(n, base[1], 2, self.slots[2].at[par], 2 * b[1])
        elif k == 4:
            self.add(n, base[1] + 1 - b[2], 1, self.slots[3].at[par], 1 - b[2])
            self.exchange(4, n).start()
            self.add(n, base[2], 1, self.slots[3].at[par], b[2])
        elif k == 5:
            self.add(n, base[2], 1, self.slots[4].at[par], 0, self.kept.at[n])
            self.exchange(5, n).start()
        elif k <= 5 + self.extra:
            keep = self.kept.at[n]
            keep[base[2]] = (keep[base[2]].astype(f32) + self.slots[k - 1].at[par][0].astype(f32)).astype(bf16)
            self.exchange(k, n).start()
        elif k < self.stages - 1:
            self.exchange(k, n).start()
        else:
            self.store(n).start()

    def store(self, n):
        return pltpu.make_async_copy(self.kept.at[n], self.out.at[n], self.out_sem.at[n])

    def give(self):
        self.ready += 1

    def free(self, n):
        return n < SLOTS or self.at[n - SLOTS] > 5

    def tick(self, only=CHUNKS):
        moved = 0
        for n in range(CHUNKS):
            if self.at[n] < self.stages and (n < self.ready) and moved < only:
                if n and self.at[n - 1] < min(self.at[n] + 2, self.stages):
                    continue
                self.stage(self.at[n], n)
                self.at[n] += 1
                moved += 1

    def done(self):
        return all(a == self.stages for a in self.at)


def put_pieces(grad, n, shard, value, blocks):
    core, y = shard % 2, shard // 2
    for k in range(8):
        for c in range(3):
            col = 128 * (3 * (k // 4) + c)
            row = 48 * (k % 4)
            grad[n % SLOTS, core, y, k, 48 * c:48 * c + 48, :] = value[row:row + 48, col:col + 128]


def backward_kernel(reps, len_ref, gain_ref, x_in, cot_in, mid_in, q_in, k_in, v_in, a_in, log_in, cos_in, sin_in,
                    wq_in, wo_in, wf_in, wd_in,
                    block_out, input_grad, grad_out, gain_out,
                    mid_s, dmid_s, dy_s, x_s, cos_s, sin_s, wq_s, wo_s, out_s,
                    grad_s, kept_s, gain_s, send_sem, recv_sem, gsend_sem, grecv_sem, out_sem, load_sem, store_sem, *slots):
    count, width = x_s.shape
    rows = width // 4
    blocks = count // BLK
    rep, fs = lax.axis_index("rep"), lax.axis_index("fsdp")
    ids = partners(rep, fs, reps)
    bits = reps.bit_length() - 1
    names = ("core", "y") + tuple("bit%d" % b for b in range(bits))
    red = Reduce(ids, reps, grad_s, slots, kept_s, grad_out, (send_sem, recv_sem), out_sem)
    ends = seq_ends(len_ref)
    valid = ends[3]

    def load(i, src, dst):
        c = pltpu.make_async_copy(src, dst, load_sem.at[i])
        c.start()
        return c

    g1, g2 = gain_ref[0:1, :], gain_ref[1:2, :]

    def feed(wf_s, wd_s, h2_s, h2t_s, z_s, df_s):
        need = [load(0, mid_in, mid_s), load(1, cot_in, dy_s)]
        wait_w = []
        for j in range(4):
            wait_w.append((load(2 + 2 * j, wf_in.at[pl.ds(8 * j, 8)], wf_s.at[pl.ds(8 * j, 8)]),
                           load(3 + 2 * j, wd_in.at[j], wd_s.at[j])))
        late = [load(10, x_in, x_s), load(11, cos_in, cos_s), load(12, sin_in, sin_s), load(13, wq_in, wq_s),
                load(14, wo_in, wo_s)]
        meet(ids, names)
        for c in need:
            c.wait()

        @pl.loop(0, blocks)
        def _(i):
            blk = rows_of(i)
            unit, _ = unit_rows(mid_s[blk, :])
            h2_s[blk, :] = (unit * g2).astype(bf16)
            token = lax.broadcasted_iota(jnp.int32, (BLK, 1), 0) + i * BLK
            dy_s[blk, :] = jnp.where(token < valid, dy_s[blk, :], 0)
        h2t_s[...] = h2_s[...].T

        for j in range(4):
            for c in wait_w[j]:
                c.wait()

            @pl.loop(0, blocks)
            def _(i):
                blk = rows_of(i)
                h2 = h2_s[blk, :]
                gate = dot(h2, joined(wf_s, 8 * j, 4), 1, 0)
                up = dot(h2, joined(wf_s, 8 * j + 4, 4), 1, 0)
                dz = dot(dy_s[blk, :], wd_s[j], 1, 1)
                sg = 1.0 / (1.0 + jnp.exp(-gate))
                silu = gate * sg
                z = (silu * up).astype(bf16)
                z_s[blk, :] = z
                dgate = (dz * up * (sg * (1.0 + gate * (1.0 - sg)))).astype(bf16)
                dup = (dz * silu).astype(bf16)
                df_s[blk, 0:512] = dgate
                df_s[blk, 512:1024] = dup
                add = dot(z, wd_s[j], 1, 0)
                back = dot(jnp.concatenate([dgate, dup], axis=1), joined(wf_s, 8 * j, 8), 1, 1)
                if j == 0:
                    out_s[blk, :] = mid_s[blk, :] + add
                    dmid_s[blk, :] = back
                else:
                    out_s[blk, :] += add
                    dmid_s[blk, :] += back
            for s in range(4):
                core, y = s % 2, s // 2
                gwd = dot(z_s[:, 128 * s:128 * s + 128], dy_s[...], 0, 0).astype(bf16)
                for k in range(8):
                    for c in range(6):
                        grad_s[2 * j, core, y, k, 16 * c:16 * c + 16, :] = gwd[16 * k:16 * k + 16, 128 * c:128 * c + 128]
                gwf = dot(h2t_s[rows * s:rows * s + rows, :], df_s[...], 1, 0).astype(bf16)
                for k in range(8):
                    grad_s[2 * j, core, y, k, 96:144, :] = gwf[0:48, 128 * k:128 * k + 128]
                    grad_s[2 * j + 1, core, y, k, 0:144, :] = gwf[48:192, 128 * k:128 * k + 128]
            red.give()
            red.give()
            red.tick()
        for c in late:
            c.wait()

    V = pltpu.VMEM
    pl.run_scoped(feed, V((32, width, 128), bf16), V((4, FF // 4, width), bf16), V((count, width), bf16),
                  V((width, count), bf16), V((count, 512), bf16), V((count, 1024), bf16))

    def attention(q_s, k_s, v_s, kt_s, a_s, da_s, log_s, dmb_s, dq3_s, h1t_s, bias, dqt_s):
        need = [load(0, q_in, q_s), load(1, k_in, k_s), load(2, v_in, v_s), load(3, log_in, log_s), load(4, a_in, a_s)]

        gain_s[...] = jnp.zeros_like(gain_s)
        @pl.loop(0, blocks)
        def _(i):
            blk = rows_of(i)
            unit, inverse = unit_rows(mid_s[blk, :])
            dh = dmid_s[blk, :]
            gain_s[0, 1:2, :] += jnp.sum(dh * unit, axis=0, keepdims=True)
            scaled = dh * g2
            dmid = dy_s[blk, :].astype(f32) + inverse * (scaled - unit * jnp.mean(scaled * unit, axis=-1, keepdims=True))
            dmid_s[blk, :] = dmid
            dmb_s[blk, :] = dmid.astype(bf16)
            mid_s[blk, :] = out_s[blk, :]
        red.tick()
        for c in need:
            c.wait()

        @pl.loop(0, 3)
        def _(c):
            part = pl.ds(pl.multiple_of(c * 256, 256), 256)
            weight = jnp.concatenate([wo_s[i, part, :] for i in range(6)], axis=1)
            da = dot(dmb_s[...], weight, 1, 1).astype(bf16)
            da_s[2 * c] = da[:, 0:128]
            da_s[2 * c + 1] = da[:, 128:256]
        for s in range(4):
            assert red.free(8)
            gwo = dot(a_s[:, rows * s:rows * s + rows], dmb_s[...], 0, 0).astype(bf16)
            put_pieces(grad_s, 8, s, gwo, 6)
        red.give()
        red.tick()

        @pl.loop(0, blocks)
        def _(i):
            blk = rows_of(i)
            unit, _ = unit_rows(x_s[blk, :].astype(f32))
            da_unit = (unit * g1).astype(bf16)
            dmb_s[blk, :] = da_unit
        h1t_s[...] = dmb_s[...].T
        fill_bias(ends, bias, count)

        def pair(p, place):
            kt_s[...] = k_s[p].T
            cols = pl.ds(pl.multiple_of(p * 128, 128), 128)
            product = da_s[p].astype(f32) * a_s[:, cols].astype(f32)
            pick = ((lax.broadcasted_iota(jnp.int32, (8, 128), 1) // 64)
                    == lax.broadcasted_iota(jnp.int32, (8, 128), 0)).astype(bf16)
            high = product.astype(bf16)
            low = (product - high.astype(f32)).astype(bf16)
            centred = dot(pick, high, 1, 1) + dot(pick, low, 1, 1)

            def first(j, h):
                lo = j * BLK
                q, da = q_s[p, lo:, :], da_s[p, lo:, :]
                mine = lane_head(h, q.shape)
                q, da = jnp.where(mine, q, 0), jnp.where(mine, da, 0)
                return dot(k_s[p, lo:lo + BLK, :], q, 1, 1), dot(v_s[p, lo:lo + BLK, :], da, 1, 1), q, da

            def middle(j, h, s, dp):
                lo = j * BLK
                weight = jnp.exp2(s + bias[lo:lo + BLK, lo:] - log_s[p, h:h + 1, lo:])
                ds = (weight * (dp - centred[h:h + 1, lo:])).astype(bf16)
                return weight.astype(bf16), ds

            sums = {}

            def last(j, h, weight, ds, q, da):
                lo = j * BLK
                dv, dk = dot(weight, da, 1, 0), dot(ds, q, 1, 0)
                dq = dot(kt_s[64 * h:64 * h + 64, lo:lo + BLK], ds, 1, 0)
                if j == 0:
                    dqt_s[64 * h:64 * h + 64, :] = dq
                else:
                    dqt_s[64 * h:64 * h + 64, lo:] += dq
                if j in sums:
                    dk, dv = dk + sums[j][0], dv + sums[j][1]
                    dk = rope(dk * (1.0 / LOG2E), cos_s[lo:lo + BLK, :], sin_s[lo:lo + BLK, :], -1)
                    dq3_s[place + 2, lo:lo + BLK, :] = dk.astype(bf16)
                    dq3_s[place + 4, lo:lo + BLK, :] = dv.astype(bf16)
                else:
                    sums[j] = (dk, dv)

            tasks = [(j, h) for j in range(blocks) for h in range(2)]
            now = first(*tasks[0])
            held = None
            for n, task in enumerate(tasks):
                ahead = first(*tasks[n + 1]) if n + 1 < len(tasks) else None
                pd = middle(*task, now[0], now[1])
                if held is not None:
                    last(*held)
                held = (*task, *pd, now[2], now[3])
                now = ahead
            last(*held)
            dq3_s[place] = rope(dqt_s[...].T * 0.125, cos_s[...], sin_s[...], -1).astype(bf16)

        for c in range(3):
            @pl.loop(0, 2)
            def _(i):
                pair(2 * c + i, 6 * c + i)
            assert red.free(9 + c)
            columns = joined(dq3_s, 6 * c, 6)
            for s in range(4):
                gwq = dot(h1t_s[rows * s:rows * s + rows, :], columns, 1, 0).astype(bf16)
                put_pieces(grad_s, 9 + c, s, gwq, 6)
            red.give()
            red.tick()
            red.tick()

        @pl.loop(0, blocks)
        def _(i):
            blk = rows_of(i)
            dq3 = jnp.concatenate([dq3_s[n, blk, :] for n in range(18)], axis=1)
            dh = dot(dq3, joined(wq_s, 0, 18), 1, 1)
            unit, inverse = unit_rows(x_s[blk, :].astype(f32))
            gain_s[0, 0:1, :] += jnp.sum(dh * unit, axis=0, keepdims=True)
            scaled = dh * g1
            dmid_s[blk, :] += inverse * (scaled - unit * jnp.mean(scaled * unit, axis=-1, keepdims=True))
            dmb_s[blk, :] = mid_s[blk, :].astype(bf16)
        a = pltpu.make_async_copy(dmid_s, input_grad, store_sem.at[0])
        b = pltpu.make_async_copy(dmb_s, block_out, store_sem.at[1])
        a.start()
        b.start()
        step = 0
        pending = None
        while not red.done() or step <= len(names):
            if pending is not None:
                pending.wait()
                gain_s[step] = gain_s[step - 1] + gain_s[len(names) + step]
                pending = None
            if step < len(names):
                pending = remote(gain_s.at[step], gain_s.at[len(names) + 1 + step], gsend_sem.at[step], grecv_sem.at[step],
                                 ids[names[step]])
                pending.start()
            step += 1
            red.tick()
        gain_out[...] = pltpu.roll(gain_s[len(names)], width - fs * rows, 1)
        a.wait()
        b.wait()

    pairs = width // 128
    pl.run_scoped(attention, V((pairs, count, 128), bf16), V((pairs, count, 128), bf16), V((pairs, count, 128), bf16),
                  V((128, count), bf16), V((count, width), bf16), V((pairs, count, 128), bf16), V((pairs, 8, count), f32),
                  V((count, width), bf16), V((18, count, 128), bf16), V((width, count), bf16), V((count, count), f32),
                  V((128, count), f32))
    for n in range(CHUNKS):
        red.store(n).wait()


def backward(reps, lengths, gain, tokens, cotangent, mid, q, k, v, a, log, cosine, sine, wq, wo, wf, wd):
    count, width = tokens.shape
    S = jax.ShapeDtypeStruct
    V = pltpu.VMEM
    dma = pltpu.SemaphoreType.DMA
    bits = reps.bit_length() - 1
    steps = 2 + bits
    exchanges = 8 + bits - 3
    slots = [V((2, 2, 8, PIECE, 128), bf16), V((2, 8, PIECE, 128), bf16), V((2, 4, PIECE, 128), bf16),
             V((2, 2, PIECE, 128), bf16), V((2, 1, PIECE, 128), bf16)]
    slots += [V((2, 1, PIECE, 128), bf16)] * (bits - 3)
    return pl.pallas_call(
        functools.partial(backward_kernel, reps),
        name="backward_reduce",
        in_specs=[SM, VM] + [ANY] * 14,
        out_specs=[ANY] * 3 + [VM],
        out_shape=[S((count, width), bf16), S((count, width), f32), S((CHUNKS, 8, PIECE, 128), bf16), S((8, width), f32)],
        scratch_shapes=[
            V((count, width), f32), V((count, width), f32), V((count, width), bf16), V((count, width), bf16),
            V((count, 128), f32), V((count, 128), f32), V((18, width, 128), bf16), V((6, width, 128), bf16),
            V((count, width), f32),
            V((SLOTS, 2, 2, 8, PIECE, 128), bf16), V((CHUNKS, 8, PIECE, 128), bf16), V((2 * steps + 1, 8, width), f32),
            dma((exchanges, 2)), dma((exchanges, 2)), dma((steps,)), dma((steps,)), dma((CHUNKS,)), dma((15,)), dma((2,))] + slots,
        compiler_params=pltpu.CompilerParams(collective_id=1, has_side_effects=True, vmem_limit_bytes=62 * 2**20),
    )(lengths, gain, tokens, cotangent, mid, q, k, v, a, log, cosine, sine, wq, wo, wf, wd)


def adamw(weight, first, second, grad, rate):
    first_new = beta_first * first + (1.0 - beta_first) * grad
    second_new = beta_second * second + (1.0 - beta_second) * grad * grad
    first_hat = first_new * (1.0 / (1.0 - beta_first**STEP))
    second_hat = second_new * (1.0 / (1.0 - beta_second**STEP))
    return (
        first_new,
        second_new,
        weight - rate * (first_hat / (jnp.sqrt(second_hat) + adam_eps) + decay_rate * weight),
    )


def update_tasks(width):
    rows = width // 4
    tasks = []
    for t in range(3):
        cols = [[(9 + c, r + 4 * ((2 * t + i) // 3), 48 * ((2 * t + i) % 3), 48) for r in range(4)]
                for c in range(3) for i in range(2)]
        tasks.append((0, (0, rows), t * width, cols))
    for k in range(8):
        tasks.append((2, (0, rows), 512 * k, [[(2 * j, k, 96, 48), (2 * j + 1, k, 0, 144)] for j in range(4)]))
    for j in range(4):
        tasks.append((3, (128 * j, 128), 0, [[(2 * j, k, 16 * c, 16) for k in range(8)] for c in range(6)]))
    tasks.append((1, (0, rows), 0, [[(8, r + 4 * (b // 3), 48 * (b % 3), 48) for r in range(4)] for b in range(6)]))
    return tasks


def update_kernel(rates, tasks, depth, grad_ref, gain_grad, *refs):
    state, refs = refs[:12], refs[12:]
    gain_state, refs = refs[:3], refs[3:]
    new, refs = refs[:12], refs[12:]
    gain_new, refs = refs[:3], refs[3:]
    taken, made, in_sem, out_sem = refs

    def moves(n, out):
        w, (row, rows), col, cols = tasks[n]
        wide = 128 * len(cols)
        slot = n % depth
        found = []
        for i in range(3):
            if out:
                found.append(pltpu.make_async_copy(made.at[slot, i, pl.ds(0, rows), pl.ds(0, wide)],
                                                   new[3 * w + i].at[pl.ds(row, rows), pl.ds(col, wide)], out_sem.at[slot, i]))
            else:
                found.append(pltpu.make_async_copy(state[3 * w + i].at[pl.ds(row, rows), pl.ds(col, wide)],
                                                   taken.at[slot, i, pl.ds(0, rows), pl.ds(0, wide)], in_sem.at[slot, i]))
        return found

    for n in range(depth):
        for c in moves(n, False):
            c.start()
    columns = gain_grad[0:2, 0:gain_new[0].shape[1]]
    for ref, value in zip((gain_new[1], gain_new[2], gain_new[0]), adamw(gain_state[0][...], gain_state[1][...], gain_state[2][...], columns, 1.0)):
        ref[...] = value
    for n, (w, (_, rows), _, cols) in enumerate(tasks):
        slot = n % depth
        for c in moves(n, False):
            c.wait()
        if n >= depth:
            for c in moves(n - depth, True):
                c.wait()
        for i, pieces in enumerate(cols):
            grad = jnp.concatenate([grad_ref[c, p, r:r + m, :] for c, p, r, m in pieces], axis=0).astype(f32)
            lanes = slice(128 * i, 128 * i + 128)
            held = [taken[slot, s, 0:rows, lanes] for s in range(3)]
            for s, value in zip((1, 2, 0), adamw(held[0], held[1], held[2], grad, rates[w])):
                made[slot, s, 0:rows, lanes] = value
        for c in moves(n, True):
            c.start()
        if n + depth < len(tasks):
            for c in moves(n + depth, False):
                c.start()
    for n in range(len(tasks) - depth, len(tasks)):
        for c in moves(n, True):
            c.wait()


def update(rates, grads, gain_grad, state, gain_state):
    width = gain_grad.shape[1]
    S = jax.ShapeDtypeStruct
    depth = 3
    dma = pltpu.SemaphoreType.DMA
    return pl.pallas_call(
        functools.partial(update_kernel, rates, update_tasks(width), depth),
        name="update",
        in_specs=[VM, VM] + [ANY] * 12 + [VM] * 3,
        out_specs=[ANY] * 12 + [VM] * 3,
        out_shape=[S(z.shape, f32) for z in state + gain_state],
        scratch_shapes=[pltpu.VMEM((depth, 3, width // 4, width), f32), pltpu.VMEM((depth, 3, width // 4, width), f32),
                        dma((depth, 3)), dma((depth, 3))],
        compiler_params=pltpu.CompilerParams(vmem_limit_bytes=60 * 2**20),
    )(grads, gain_grad, *state, *gain_state)


def shards(reps, tokens, cotangent, lengths, w_qkv, m_qkv, v_qkv, w_proj, m_proj, v_proj, w_ffn, m_ffn, v_ffn,
           w_down, m_down, v_down, gains, m_gains, v_gains):
    count, width = tokens.shape
    wq, wo, wf, wd, q, k, v, a, log, mid, gain, cosine, sine = forward(
        reps, lengths, tokens, gains, w_qkv, w_proj, w_ffn, w_down)
    block_out, input_grad, grads, gain_grad = backward(
        reps, lengths, gain, tokens, cotangent, mid, q, k, v, a, log, cosine, sine, wq, wo, wf, wd)
    wide = 3.0 * width ** (-0.5)
    proj = 3.0 * (count / (10.0 * width)) ** 0.5
    down = 6.0 * FF ** (-0.5)
    new = update(
        (wide, proj, wide, down), grads, gain_grad,
        (w_qkv, m_qkv, v_qkv, w_proj, m_proj, v_proj, w_ffn, m_ffn, v_ffn, w_down, m_down, v_down),
        (gains, m_gains, v_gains))
    return (block_out, input_grad) + tuple(new[3 * w + s] for w in range(5) for s in (1, 2, 0))


def solution(mesh):
    reps = mesh.shape["rep"]
    tokens = P(("rep", "fsdp"), None)
    weight = P("fsdp", None)
    gain = P(None, "fsdp")
    return jax.shard_map(
        functools.partial(shards, reps),
        mesh=mesh,
        in_specs=(tokens,) * 3 + (weight,) * 12 + (gain,) * 3,
        out_specs=(tokens,) * 2 + (weight,) * 12 + (gain,) * 3,
        check_vma=False,
    )
```

```python
import functools

import jax
import jax.numpy as jnp
import numpy as np
from jax import lax
from jax.experimental import pallas as pl
from jax.experimental.pallas import tpu as pltpu
from jax.sharding import PartitionSpec as P

HEADS = 12
FF = 2048
STEP = 10
norm_eps = 1e-05
rope_base = 10000.0
beta_first = 0.9
beta_second = 0.95
adam_eps = 1e-08
decay_rate = 0.1
LOG2E = 1.4426950408889634
MASKED = -1e30
MESH = pl.DeviceIdType.MESH
f32 = jnp.float32
bf16 = jnp.bfloat16
BLK = 256
CHUNKS = 12
PIECE = 144
SLOTS = 9
LAGS = (2, 2, 2, 2, 2)
ANY = pl.BlockSpec(memory_space=pl.ANY)
VM = pl.BlockSpec(memory_space=pltpu.VMEM)
SM = pl.BlockSpec(memory_space=pltpu.SMEM)


def dot(a, b, ca, cb):
    return lax.dot_general(a, b, (((ca,), (cb,)), ((), ())), preferred_element_type=f32)


def joined(ref, first, number):
    return jnp.concatenate([ref[first + i] for i in range(number)], axis=1)


def rows_of(i):
    return pl.ds(pl.multiple_of(i * BLK, BLK), BLK)


def lane_head(h, shape):
    return (lax.broadcasted_iota(jnp.int32, shape, 1) // 64) == h


def seq_ends(len_ref):
    total = 0
    ends = []
    for j in range(4):
        total = total + len_ref[0, j]
        ends.append(total)
    return ends


def fill_bias(ends, bias, count):
    q = lax.broadcasted_iota(jnp.int32, (1, count), 1)
    sq = sum((q >= e).astype(jnp.int32) for e in ends)

    @pl.loop(0, count // BLK)
    def _(j):
        k = lax.broadcasted_iota(jnp.int32, (BLK, 1), 0) + j * BLK
        sk = sum((k >= e).astype(jnp.int32) for e in ends)
        bias[rows_of(j), :] = jnp.where((sk == sq) & (k <= q), 0.0, MASKED)


def rope(block, cosine, sine, sign):
    lane = lax.broadcasted_iota(jnp.int32, block.shape, 1)
    swapped = jnp.where(lane % 64 < 32, pltpu.roll(block, 96, 1), pltpu.roll(block, 32, 1))
    if sign > 0:
        return block * cosine + swapped * sine
    return block * cosine - swapped * sine


def remote(src, dst, send_sem, recv_sem, device):
    return pltpu.make_async_remote_copy(
        src_ref=src, dst_ref=dst, send_sem=send_sem, recv_sem=recv_sem,
        device_id=device, device_id_type=MESH)


def unit_rows(value):
    inverse = lax.rsqrt(jnp.mean(value * value, axis=-1, keepdims=True) + norm_eps)
    return value * inverse, inverse


class Gather:
    def __init__(self, own, full, first, blocks, shard_rows, sems, index, ids, direct=False):
        self.direct = direct
        self.own, self.full, self.first, self.blocks, self.n = own, full, first, blocks, shard_rows
        self.ssem, self.rsem, self.w, self.ids = sems[0], sems[1], index, ids
        rep, fs = ids["rep"], ids["fsdp"]
        self.b0, self.b1 = rep % 2, (rep // 2) % 2
        self.q = rep % 4
        self.far = (fs + 2) % 4
        self.fs = fs
        self.quarter = shard_rows // 4

    def part(self, shard, quarter, quarters, half=None):
        row = pl.multiple_of(shard * self.n + quarter * self.quarter, 16)
        first, blocks = self.first, self.blocks
        if half is not None:
            blocks = blocks // 2
            first = first + half * blocks
        return self.full.at[pl.ds(first, blocks), pl.ds(row, quarters * self.quarter), :]

    def cp(self, i, ref, device, src=None):
        return remote(ref if src is None else src, ref, self.ssem.at[self.w, i], self.rsem.at[self.w, i], device)

    def copy(self, i):
        d = self.ids
        p, far, fs, q = self.part, self.far, self.fs, self.q
        q1 = (1 - self.b0) + 2 * self.b1
        q2 = self.b0 + 2 * (1 - self.b1)
        q3 = (1 - self.b0) + 2 * (1 - self.b1)
        own = own_quarter = None
        if self.own is not None:
            own = self.own.at[pl.ds(self.first, self.blocks)]
            own_quarter = self.own.at[pl.ds(self.first, self.blocks), pl.ds(pl.multiple_of(q * self.quarter, 16), self.quarter), :]
        if self.direct and i:
            return self.cp(i, p(fs if i == 1 else far, 0, 4), d["y" if i == 1 else "core"])
        return [
            lambda: self.cp(0, p(fs, 0, 4), d["core"], own),
            lambda: self.cp(1, p(fs, q, 1), d["y"], own_quarter),
            lambda: self.cp(2, p(far, q, 1, 0), d["bit0"]),
            lambda: self.cp(3, p(far, q, 1, 1), d["bit1"]),
            lambda: self.cp(4, p(far, q, 1), d["core"]),
            lambda: self.cp(5, p(far, 2 * self.b1, 2, 0), d["bit1"]),
            lambda: self.cp(6, p(far, q, 1, 1), d["bit0"]),
            lambda: self.cp(7, p(far, q2, 1, 1), d["bit0"]),
            lambda: self.cp(8, p(far, q1, 1, 0), d["core"]),
            lambda: self.cp(9, p(far, q2, 1, 1), d["core"]),
            lambda: self.cp(10, p(far, 2 * (1 - self.b1), 2, 0), d["core"]),
            lambda: self.cp(11, p(far, q1, 1, 1), d["core"]),
            lambda: self.cp(12, p(far, q3, 1, 1), d["core"]),
        ][i]()

    def step(self, waits, starts):
        for i in waits:
            self.copy(i).wait_recv()
        for i in starts:
            self.copy(i).start()

    def start(self):
        self.step((), (1, 0))

    def second(self):
        self.step((1,), (4,) if self.direct else (2, 3, 4))

    def third(self):
        self.step((2, 3), (5, 6, 7, 8, 9))

    def fourth(self):
        self.step((5, 6, 7), (10, 11, 12))

    def arrive(self):
        self.step((0, 4) if self.direct else (0, 4, 8, 9, 10, 11, 12), ())

    def sent(self):
        for i in (0, 1, 4) if self.direct else range(13):
            self.copy(i).wait_send()


def partners(rep, fs, reps):
    found = {"rep": rep, "fsdp": fs, "core": (rep, fs ^ 1), "y": (rep, fs ^ 2)}
    for b in range(reps.bit_length() - 1):
        found["bit%d" % b] = (rep ^ (1 << b), fs)
    for d in (1, 2, 3):
        found["z%d" % d] = (rep ^ (2 * (d // 2) + 4 * (d % 2)), fs)
    return found


def meet(ids, names):
    barrier = pltpu.get_barrier_semaphore()
    for name in names:
        pl.semaphore_signal(barrier, inc=1, device_id=ids[name], device_id_type=MESH)
    pl.semaphore_wait(barrier, len(names))


def place_gains(ref, rows, fs):
    ref[...] = pltpu.roll(ref[...], fs * rows, 1)


def forward_kernel(reps, len_ref, x_in, gain_in, freq_ref, wq_in, wo_in, wf_in, wd_in,
                   wq_out, wo_out, wf_out, wd_out, q_out, k_out, v_out, a_out, at_out, h1t_out, log_out, mid_out, gain_out, cos_out, sin_out,
                   wq_s, wo_s, st_q, st_o, st_f, st_d, own_f, own_d, gain_a, gain_b, gain_c, x_s, cos_s, sin_s,
                   h1_s, h1t_s, q_s, k_s, vt_s, v_s, a_s, at_s, log_s, mid_s, bias,
                   load_sem, store_sem, send_sem, recv_sem, gsend_sem, grecv_sem):
    count, width = x_s.shape
    pairs = width // 128
    rows = width // 4
    rep, fs = lax.axis_index("rep"), lax.axis_index("fsdp")
    ids = partners(rep, fs, reps)
    load_q = pltpu.make_async_copy(wq_in, st_q, load_sem.at[0])
    load_x = pltpu.make_async_copy(x_in, x_s, load_sem.at[1])
    load_o = pltpu.make_async_copy(wo_in, st_o, load_sem.at[2])
    load_f = pltpu.make_async_copy(wf_in, st_f, load_sem.at[3])
    load_d = pltpu.make_async_copy(wd_in, st_d, load_sem.at[4])
    for c in (load_q, load_x, load_o, load_f, load_d):
        c.start()
    gain_a[...] = jnp.zeros_like(gain_a)
    gain_a[0:2, 0:rows] = gain_in[...].astype(bf16).astype(f32)
    gain_a[...] = pltpu.roll(gain_a[...], fs * rows, 1)
    meet(ids, ("core", "y", "bit0", "bit1"))

    sems = (send_sem, recv_sem)
    near = [Gather(None, wq_s, 6 * c, 6, rows, sems, c, ids, c == 0) for c in range(3)]
    proj = Gather(None, wo_s, 0, 6, rows, sems, 3, ids)
    wide = [Gather(own_f, wf_out, 8 * j, 8, rows, sems, 4 + j, ids) for j in range(4)]
    down = Gather(own_d, wd_out, 0, 4, FF // 16, sems, 8, ids)

    g_core = remote(gain_a, gain_b, gsend_sem.at[0], grecv_sem.at[0], ids["core"])
    g_core.start()
    own_rows = pl.ds(pl.multiple_of(fs * rows, 16), rows)
    load_q.wait()
    for c in range(3):
        for t in range(3):
            for i in range(2):
                col = t * width + (2 * c + i) * 128
                wq_s[6 * c + 2 * t + i, own_rows, :] = st_q[:, col:col + 128].astype(bf16)
        if c < 2:
            near[c].start()
    load_o.wait()
    load_f.wait()
    for j in range(4):
        for n in range(8):
            col = (4 * n + j) * 128
            own_f[8 * j + n] = st_f[:, col:col + 128].astype(bf16)
    for i in range(6):
        wo_s[i, own_rows, :] = st_o[:, 128 * i:128 * i + 128].astype(bf16)
    load_d.wait()
    for j in range(4):
        own_d[j] = st_d[128 * j:128 * j + 128, :].astype(bf16)
    g_core.wait()
    gain_c[0] = gain_a[...] + gain_b[...]
    g_y = remote(gain_c.at[0], gain_c.at[1], gsend_sem.at[1], grecv_sem.at[1], ids["y"])
    g_y.start()
    near[1].second()
    near[2].start()
    wide[0].start()
    stores = [
        pltpu.make_async_copy(own_f, wf_out.at[:, own_rows, :], store_sem.at[0]),
        pltpu.make_async_copy(own_d, wd_out.at[:, pl.ds(pl.multiple_of(fs * (FF // 16), 16), FF // 16), :], store_sem.at[1]),
    ]
    for c in stores:
        c.start()
    ends = seq_ends(len_ref)
    token = lax.broadcasted_iota(jnp.int32, (1, count), 1)
    start = jnp.zeros((1, count), jnp.int32)
    for e in ends:
        start = jnp.where(token >= e, e, start)
    angle = freq_ref[:, 0:1] * (token - start).astype(f32)
    cosine, sine = jnp.cos(angle), jnp.sin(angle)
    cos_s[...] = jnp.concatenate([cosine] * 4, axis=0).T
    sin_s[...] = jnp.concatenate([-sine, sine, -sine, sine], axis=0).T
    near[2].second()
    wide[1].start()
    proj.start()
    near[1].third()
    g_y.wait()
    gain_out[...] = gain_c[0] + gain_c[1]
    g1 = gain_out[0:1, :]
    load_x.wait()

    @pl.loop(0, count // BLK)
    def _(i):
        blk = pl.ds(pl.multiple_of(i * BLK, BLK), BLK)
        x = x_s[blk, :].astype(f32)
        inverse = lax.rsqrt(jnp.mean(x * x, axis=-1, keepdims=True) + norm_eps)
        h1 = x * inverse * g1
        h1_s[blk, :] = h1.astype(bf16)
        h1t_s[:, blk] = h1.T.astype(bf16)

    near[0].second()
    wide[0].second()
    wide[2].start()
    near[2].third()
    fill_bias(ends, bias, count)
    near[1].fourth()
    wide[3].start()

    def project(c):
        h1 = h1_s[...]
        for t in range(3):
            block = dot(h1, joined(wq_s, 6 * c + 2 * t, 2), 1, 0)
            for i in range(2):
                p = 2 * c + i
                piece = block[:, 128 * i:128 * i + 128]
                if t == 0:
                    q_s[p] = (rope(piece, cos_s[...], sin_s[...], 1) * (LOG2E / 8)).astype(bf16)
                elif t == 1:
                    k_s[p] = rope(piece, cos_s[...], sin_s[...], 1).astype(bf16)
                else:
                    v_s[p] = piece.astype(bf16)
                    vt_s[p] = piece.T.astype(bf16)

    def scores(p, i, h):
        q = q_s[p, i * BLK:(i + 1) * BLK, :]
        return dot(k_s[p, :BLK * (i + 1), :], jnp.where(lane_head(h, q.shape), q, 0), 1, 1)

    def soft(p, i, h, s):
        s = s + bias[:BLK * (i + 1), i * BLK:(i + 1) * BLK]
        largest = jnp.max(s, axis=0, keepdims=True)
        e = jnp.exp2(s - largest)
        total = jnp.sum(e, axis=0, keepdims=True)
        log_s[p, h:h + 1, i * BLK:(i + 1) * BLK] = largest + jnp.log2(total)
        return e.astype(bf16), total

    def mix(p, i, h, e, total):
        return dot(vt_s[p, 64 * h:64 * h + 64, :BLK * (i + 1)], e, 1, 0) * (1.0 / total)

    def attend(p):
        tasks = [(i, h) for i in range(count // BLK) for h in range(2)]
        s = scores(p, *tasks[0])
        held = None
        outs = {}
        for n, task in enumerate(tasks):
            ahead = scores(p, *tasks[n + 1]) if n + 1 < len(tasks) else None
            weighted = soft(p, *task, s)
            if held is not None:
                outs[held[0]] = mix(p, *held[0], *held[1])
            held = (task, weighted)
            s = ahead
        outs[held[0]] = mix(p, *held[0], *held[1])
        cols = pl.ds(pl.multiple_of(p * 128, 128), 128)
        for i in range(count // BLK):
            both = jnp.concatenate([outs[i, 0], outs[i, 1]], axis=0)
            at_s[cols, i * BLK:(i + 1) * BLK] = both.astype(bf16)
            a_s[i * BLK:(i + 1) * BLK, cols] = both.T.astype(bf16)

    ready = [pltpu.make_async_copy(src, dst, store_sem.at[3 + i]) for i, (src, dst) in enumerate((
        (wq_s, wq_out), (q_s, q_out), (k_s, k_out), (v_s, v_out), (cos_s, cos_out), (sin_s, sin_out), (h1t_s, h1t_out)))]
    arrivals = [[near[0].arrive], [near[1].arrive], [near[2].arrive]]
    projected = [
        [near[2].fourth, wide[1].second, wide[0].third, down.start],
        [down.second, proj.third],
        [c.start for c in ready],
    ]
    attended = [
        [wide[1].third, wide[2].second, proj.second],
        [wide[0].fourth, wide[3].second, wide[2].third],
        [wide[1].fourth, wide[3].third],
        [wide[2].fourth, down.third, proj.fourth],
        [wide[3].fourth],
        [down.fourth],
    ]

    def at_turn(c, lists):
        for turn, steps in enumerate(lists):
            if steps:
                @pl.when(c == turn)
                def _():
                    for step in steps:
                        step()

    @pl.loop(0, 3)
    def _(c):
        at_turn(c, arrivals)
        project(c)
        at_turn(c, projected)

        @pl.loop(2 * c, 2 * c + 2)
        def _(p):
            attend(p)
            at_turn(p, attended)
    stores += ready
    proj.arrive()
    for i, (src, dst) in enumerate(((wo_s, wo_out), (a_s, a_out), (at_s, at_out), (log_s, log_out))):
        c = pltpu.make_async_copy(src, dst, store_sem.at[10 + i])
        c.start()
        stores.append(c)

    @pl.loop(0, count // BLK)
    def _(i):
        blk = pl.ds(pl.multiple_of(i * BLK, BLK), BLK)
        mid_s[blk, :] = x_s[blk, :].astype(f32) + dot(a_s[blk, :], joined(wo_s, 0, 6), 1, 0)
    c = pltpu.make_async_copy(mid_s, mid_out, store_sem.at[14])
    c.start()
    stores.append(c)
    for g in wide + [down]:
        g.arrive()
    for g in near + [proj] + wide + [down]:
        g.sent()
    for c in stores:
        c.wait()


def frequencies():
    half = 32
    frequency = rope_base ** (-2.0 * np.arange(half) / (2 * half))
    return jnp.asarray(np.broadcast_to(frequency[:, None], (half, 128)), f32)


def forward(reps, lengths, tokens, gains, w_qkv, w_proj, w_ffn, w_down):
    count, width = tokens.shape
    pairs = width // 128
    S = jax.ShapeDtypeStruct
    V = pltpu.VMEM
    rows = width // 4
    dma = pltpu.SemaphoreType.DMA
    return pl.pallas_call(
        functools.partial(forward_kernel, reps),
        name="gather_forward",
        in_specs=[SM, ANY, VM, VM, ANY, ANY, ANY, ANY],
        out_specs=[ANY] * 12 + [VM] + [ANY] * 2,
        out_shape=[S((18, width, 128), bf16), S((6, width, 128), bf16), S((32, width, 128), bf16), S((4, FF // 4, width), bf16),
                   S((pairs, count, 128), bf16), S((pairs, count, 128), bf16), S((pairs, count, 128), bf16),
                   S((count, width), bf16), S((width, count), bf16), S((width, count), bf16), S((pairs, 8, count), f32),
                   S((count, width), f32), S((8, width), f32),
                   S((count, 128), f32), S((count, 128), f32)],
        scratch_shapes=[
            V((18, width, 128), bf16), V((6, width, 128), bf16), V((rows, 3 * width), f32), V((rows, width), f32),
            V((rows, 2 * FF), f32), V((FF // 4, width), f32), V((32, rows, 128), bf16), V((4, FF // 16, width), bf16),
            V((8, width), f32), V((8, width), f32), V((2, 8, width), f32),
            V((count, width), bf16), V((count, 128), f32), V((count, 128), f32),
            V((count, width), bf16), V((width, count), bf16), V((pairs, count, 128), bf16), V((pairs, count, 128), bf16),
            V((pairs, 128, count), bf16), V((pairs, count, 128), bf16), V((count, width), bf16), V((width, count), bf16),
            V((pairs, 8, count), f32), V((count, width), f32), V((count, count), f32),
            dma((5,)), dma((15,)), dma((9, 13)), dma((9, 13)), dma((2,)), dma((2,))],
        compiler_params=pltpu.CompilerParams(collective_id=0, has_side_effects=True, vmem_limit_bytes=60 * 2**20),
    )(lengths, tokens, gains, frequencies(), w_qkv, w_proj, w_ffn, w_down)


class Reduce:
    def __init__(self, ids, reps, grad, slots, kept, out, sems, out_sem):
        self.ids = ids
        self.grad, self.slots, self.kept, self.out = grad, slots, kept, out
        self.ssem, self.rsem = sems
        self.out_sem = out_sem
        rep, fs = ids["rep"], ids["fsdp"]
        self.core, self.y = fs % 2, fs // 2
        self.half = rep % 2
        self.z = 2 * (rep // 2 % 2) + rep // 4 % 2
        self.extra = reps.bit_length() - 1 - 3
        self.stages = 7 + self.extra
        self.offsets = stage_offsets(reps)
        self.lags = stage_lags(reps)

    def cp(self, kind, par, src, dst, device):
        return remote(src, dst, self.ssem.at[kind, par], self.rsem.at[kind, par], self.ids[device])

    def exchange(self, k, n):
        g = self.grad.at[n % SLOTS]
        mine = g.at[self.core, self.y]
        keep = self.kept.at[n]
        par = n % (2 * self.lags[k])
        first = 4 * self.half
        own = keep.at[pl.ds(first + self.z, 1)]
        if k == 0:
            return [self.cp(0, par, g.at[1 - self.core], self.slots[0].at[par], "core")]
        if k == 1:
            return [self.cp(1, par, g.at[self.core, 1 - self.y], self.slots[1].at[par], "y")]
        if k == 2:
            return [self.cp(2, par, mine.at[pl.ds(4 - first, 4)], self.slots[2].at[par], "bit0")]
        if k == 3:
            return [self.cp(2 + d, par, mine.at[first + (self.z ^ d)], self.slots[3].at[par, d - 1], "z%d" % d) for d in (1, 2, 3)]
        if k < 4 + self.extra:
            return [self.cp(6 + k, par, own, self.slots[k].at[par], "bit%d" % (k - 1))]
        if k == 4 + self.extra:
            return [self.cp(5 + d, par, own, own, "z%d" % d) for d in (1, 2, 3)]
        part = keep.at[pl.ds(first, 4)]
        return [self.cp(9, par, part, part, "bit0")]

    def start(self, k, n):
        for c in self.exchange(k, n):
            c.start()

    def add(self, n, first, number, slot, offset):
        mine = self.grad.at[n % SLOTS, self.core, self.y]

        @pl.loop(0, number)
        def _(i):
            mine[first + i] = (mine[first + i].astype(f32) + slot[offset + i].astype(f32)).astype(bf16)

    def stage(self, k, n):
        par = n % (2 * self.lags[k - 1])
        first = 4 * self.half
        if k > 0:
            for c in self.exchange(k - 1, n):
                c.wait()
        if k == 0:
            self.start(0, n)
        elif k == 1:
            g, slot = self.grad.at[n % SLOTS, self.core], self.slots[0].at[par]
            for y in (1 - self.y, self.y):
                @pl.loop(0, 8)
                def _(i):
                    g[y, i] = (g[y, i].astype(f32) + slot[y, i].astype(f32)).astype(bf16)
                if y is not self.y:
                    self.start(1, n)
        elif k == 2:
            self.add(n, 4 - first, 4, self.slots[1].at[par], 4 - first)
            self.start(2, n)
            self.add(n, first, 4, self.slots[1].at[par], first)
        elif k == 3:
            self.add(n, first, 4, self.slots[2].at[par], 0)
            self.start(3, n)
        elif k == 4:
            own = first + self.z
            slot = self.slots[3].at[par]
            total = self.grad[n % SLOTS, self.core, self.y, own].astype(f32) + slot[0].astype(f32)
            self.kept[n, own] = (total + slot[1].astype(f32) + slot[2].astype(f32)).astype(bf16)
            self.start(4, n)
        elif k <= 4 + self.extra:
            own = first + self.z
            slot = self.slots[k - 1].at[par]
            self.kept[n, own] = (self.kept[n, own].astype(f32) + slot[0].astype(f32)).astype(bf16)
            self.start(k, n)
        elif k < self.stages - 1:
            self.start(k, n)
        else:
            self.store(n).start()

    def store(self, n):
        return pltpu.make_async_copy(self.kept.at[n], self.out.at[n], self.out_sem.at[n])

    def tick(self, time):
        for k in reversed(range(self.stages)):
            since = time - self.offsets[k]
            if isinstance(time, int):
                if since < 0 or (since > 8 and since % 2) or since > 2 * CHUNKS - 10:
                    continue
                self.stage(k, since if since <= 8 else (since + 8) // 2)
            else:
                late = (since + 8) // 2
                fits = jnp.logical_and(since >= 0, jnp.logical_or(since <= 8, jnp.logical_and(since == 2 * late - 8, late < CHUNKS)))

                @pl.when(fits)
                def _():
                    self.stage(k, jnp.where(since <= 8, since, late))

    def last_tick(self):
        return 2 * CHUNKS - 10 + self.offsets[-1]


def stage_offsets(reps):
    stages = 7 + reps.bit_length() - 1 - 3
    return [0] + [1 + sum(LAGS[i] if i < len(LAGS) else LAGS[-1] for i in range(k)) for k in range(stages - 1)]


def stage_lags(reps):
    offsets = stage_offsets(reps)
    return [b - a for a, b in zip(offsets, offsets[1:])]


def put_pieces(slot, value, block):
    for s in range(4):
        for i in range(2):
            half, c = divmod(block + i, 3)
            for r in range(4):
                row = 192 * s + 48 * r
                slot[s % 2, s // 2, r + 4 * half, 48 * c:48 * c + 48, :] = value[row:row + 48, 128 * i:128 * i + 128]


def backward_kernel(reps, len_ref, gain_ref, x_in, cot_in, mid_in, q_in, k_in, v_in, a_in, at_in, h1t_in, log_in, cos_in, sin_in,
                    wq_in, wo_in, wf_in, wd_in,
                    block_out, input_grad, grad_out, gain_out,
                    mid_s, dmid_s, dy_s, x_s, cos_s, sin_s, wq_s, wo_s, out_s,
                    grad_s, kept_s, gain_s, send_sem, recv_sem, gsend_sem, grecv_sem, out_sem, load_sem, store_sem, *slots):
    count, width = x_s.shape
    rows = width // 4
    blocks = count // BLK
    rep, fs = lax.axis_index("rep"), lax.axis_index("fsdp")
    ids = partners(rep, fs, reps)
    bits = reps.bit_length() - 1
    names = ("core", "y") + tuple("bit%d" % b for b in range(bits))
    friends = names[:3] + ("z1", "z2", "z3") + names[5:]
    red = Reduce(ids, reps, grad_s, slots, kept_s, grad_out, (send_sem, recv_sem), out_sem)
    ends = seq_ends(len_ref)
    valid = ends[3]

    def load(i, src, dst):
        c = pltpu.make_async_copy(src, dst, load_sem.at[i])
        c.start()
        return c

    g1, g2 = gain_ref[0:1, :], gain_ref[1:2, :]

    def feed(wf_s, wd_s, h2_s, h2t_s, z_s, df_s):
        need = [load(0, mid_in, mid_s), load(1, cot_in, dy_s)]
        def weights(j):
            return [pltpu.make_async_copy(wf_in.at[pl.ds(8 * j, 8)], wf_s.at[pl.ds(8 * j, 8)], load_sem.at[2 + 2 * j]),
                    pltpu.make_async_copy(wd_in.at[j], wd_s.at[j], load_sem.at[3 + 2 * j])]

        for j in range(4):
            for c in weights(j):
                c.start()
        late = [load(10, x_in, x_s), load(11, cos_in, cos_s), load(12, sin_in, sin_s), load(13, wq_in, wq_s),
                load(14, wo_in, wo_s)]
        meet(ids, friends)
        for c in need:
            c.wait()

        @pl.loop(0, blocks)
        def _(i):
            blk = rows_of(i)
            unit, _ = unit_rows(mid_s[blk, :])
            h2 = unit * g2
            h2_s[blk, :] = h2.astype(bf16)
            h2t_s[:, blk] = h2.T.astype(bf16)
            token = lax.broadcasted_iota(jnp.int32, (BLK, 1), 0) + i * BLK
            dy_s[blk, :] = jnp.where(token < valid, dy_s[blk, :], 0)
            out_s[blk, :] = mid_s[blk, :]
            dmid_s[blk, :] = jnp.zeros((BLK, width), f32)

        @pl.loop(0, 4)
        def _(j):
            for c in weights(j):
                c.wait()

            @pl.loop(0, blocks)
            def _(i):
                blk = rows_of(i)
                h2 = h2_s[blk, :]
                gate = dot(h2, joined(wf_s, 8 * j, 4), 1, 0)
                up = dot(h2, joined(wf_s, 8 * j + 4, 4), 1, 0)
                dz = dot(dy_s[blk, :], wd_s[j], 1, 1)
                sg = 1.0 / (1.0 + jnp.exp(-gate))
                silu = gate * sg
                z = (silu * up).astype(bf16)
                z_s[blk, :] = z
                dgate = (dz * up * (sg * (1.0 + gate * (1.0 - sg)))).astype(bf16)
                dup = (dz * silu).astype(bf16)
                df_s[blk, 0:512] = dgate
                df_s[blk, 512:1024] = dup
                out_s[blk, :] += dot(z, wd_s[j], 1, 0)
                dmid_s[blk, :] += dot(jnp.concatenate([dgate, dup], axis=1), joined(wf_s, 8 * j, 8), 1, 1)

            red.tick(2 * j - 1)
            gwd = dot(z_s[...], dy_s[...], 0, 0).astype(bf16)
            for s in range(4):
                for k in range(8):
                    for c in range(6):
                        row = 128 * s + 16 * k
                        grad_s[2 * j, s % 2, s // 2, k, 16 * c:16 * c + 16, :] = gwd[row:row + 16, 128 * c:128 * c + 128]

            @pl.loop(0, 4)
            def _(n):
                gwf = dot(h2t_s[...], df_s[:, pl.ds(pl.multiple_of(256 * n, 256), 256)], 1, 0).astype(bf16)
                for s in range(4):
                    for i in range(2):
                        lanes = slice(128 * i, 128 * i + 128)
                        grad_s[2 * j, s % 2, s // 2, 2 * n + i, 96:144, :] = gwf[rows * s:rows * s + 48, lanes]
                        grad_s[2 * j + 1, s % 2, s // 2, 2 * n + i, 0:144, :] = gwf[rows * s + 48:rows * s + rows, lanes]
            red.tick(2 * j)
        for c in late:
            c.wait()

    V = pltpu.VMEM
    pl.run_scoped(feed, V((32, width, 128), bf16), V((4, FF // 4, width), bf16), V((count, width), bf16),
                  V((width, count), bf16), V((count, 512), bf16), V((count, 1024), bf16))

    def attention(q_s, k_s, v_s, kt_s, a_s, at_s, da_s, log_s, dmb_s, dq3_s, h1t_s, bias, dqt_s):
        need = [load(0, q_in, q_s), load(1, k_in, k_s), load(2, v_in, v_s), load(3, log_in, log_s), load(4, a_in, a_s),
                load(5, at_in, at_s), load(6, h1t_in, h1t_s)]

        gain_s[...] = jnp.zeros_like(gain_s)
        @pl.loop(0, blocks)
        def _(i):
            blk = rows_of(i)
            unit, inverse = unit_rows(mid_s[blk, :])
            dh = dmid_s[blk, :]
            gain_s[0, 1:2, :] += jnp.sum(dh * unit, axis=0, keepdims=True)
            scaled = dh * g2
            dmid = dy_s[blk, :].astype(f32) + inverse * (scaled - unit * jnp.mean(scaled * unit, axis=-1, keepdims=True))
            dmid_s[blk, :] = dmid
            dmb_s[blk, :] = dmid.astype(bf16)
            mid_s[blk, :] = out_s[blk, :]
        red.tick(7)
        for c in need:
            c.wait()

        @pl.loop(0, 3)
        def _(c):
            part = pl.ds(pl.multiple_of(c * 256, 256), 256)
            weight = jnp.concatenate([wo_s[i, part, :] for i in range(6)], axis=1)
            da = dot(dmb_s[...], weight, 1, 1).astype(bf16)
            da_s[2 * c] = da[:, 0:128]
            da_s[2 * c + 1] = da[:, 128:256]
        for n in range(3):
            gwo = dot(at_s[...], dmb_s[:, 256 * n:256 * n + 256], 1, 0).astype(bf16)
            put_pieces(grad_s.at[8], gwo, 2 * n)
        red.tick(8)
        fill_bias(ends, bias, count)

        def pair(p, place):
            kt_s[...] = k_s[p].T
            cols = pl.ds(pl.multiple_of(p * 128, 128), 128)
            product = da_s[p].astype(f32) * a_s[:, cols].astype(f32)
            pick = ((lax.broadcasted_iota(jnp.int32, (8, 128), 1) // 64)
                    == lax.broadcasted_iota(jnp.int32, (8, 128), 0)).astype(bf16)
            high = product.astype(bf16)
            low = (product - high.astype(f32)).astype(bf16)
            centred = dot(pick, high, 1, 1) + dot(pick, low, 1, 1)

            def first(j, h):
                lo = j * BLK
                q, da = q_s[p, lo:, :], da_s[p, lo:, :]
                mine = lane_head(h, q.shape)
                q, da = jnp.where(mine, q, 0), jnp.where(mine, da, 0)
                return dot(k_s[p, lo:lo + BLK, :], q, 1, 1), dot(v_s[p, lo:lo + BLK, :], da, 1, 1), q, da

            def middle(j, h, s, dp):
                lo = j * BLK
                weight = jnp.exp2(s + bias[lo:lo + BLK, lo:] - log_s[p, h:h + 1, lo:])
                ds = (weight * (dp - centred[h:h + 1, lo:])).astype(bf16)
                return weight.astype(bf16), ds

            sums = {}

            def last(j, h, weight, ds, q, da):
                lo = j * BLK
                dv, dk = dot(weight, da, 1, 0), dot(ds, q, 1, 0)
                dq = dot(kt_s[64 * h:64 * h + 64, lo:lo + BLK], ds, 1, 0)
                if j == 0:
                    dqt_s[64 * h:64 * h + 64, :] = dq
                else:
                    dqt_s[64 * h:64 * h + 64, lo:] += dq
                if j in sums:
                    dk, dv = dk + sums[j][0], dv + sums[j][1]
                    dk = rope(dk * (1.0 / LOG2E), cos_s[lo:lo + BLK, :], sin_s[lo:lo + BLK, :], -1)
                    dq3_s[place + 2, lo:lo + BLK, :] = dk.astype(bf16)
                    dq3_s[place + 4, lo:lo + BLK, :] = dv.astype(bf16)
                else:
                    sums[j] = (dk, dv)

            tasks = [(j, h) for j in range(blocks) for h in range(2)]
            now = first(*tasks[0])
            held = None
            for n, task in enumerate(tasks):
                ahead = first(*tasks[n + 1]) if n + 1 < len(tasks) else None
                pd = middle(*task, now[0], now[1])
                if held is not None:
                    last(*held)
                held = (*task, *pd, now[2], now[3])
                now = ahead
            last(*held)
            dq3_s[place] = rope(dqt_s[...].T * 0.125, cos_s[...], sin_s[...], -1).astype(bf16)

        @pl.loop(0, 3)
        def _(c):
            @pl.loop(0, 2)
            def _(i):
                pair(2 * c + i, 6 * c + i)

                @pl.when(i == 0)
                def _():
                    red.tick(9 + 2 * c)
            for t in range(3):
                gwq = dot(h1t_s[...], joined(dq3_s, 6 * c + 2 * t, 2), 1, 0).astype(bf16)
                put_pieces(grad_s.at[c], gwq, 2 * t)
            red.tick(10 + 2 * c)

        @pl.loop(0, blocks)
        def _(i):
            blk = rows_of(i)
            dq3 = jnp.concatenate([dq3_s[n, blk, :] for n in range(18)], axis=1)
            dh = dot(dq3, joined(wq_s, 0, 18), 1, 1)
            unit, inverse = unit_rows(x_s[blk, :].astype(f32))
            gain_s[0, 0:1, :] += jnp.sum(dh * unit, axis=0, keepdims=True)
            scaled = dh * g1
            dmid_s[blk, :] += inverse * (scaled - unit * jnp.mean(scaled * unit, axis=-1, keepdims=True))
            dmb_s[blk, :] = mid_s[blk, :].astype(bf16)
        a = pltpu.make_async_copy(dmid_s, input_grad, store_sem.at[0])
        b = pltpu.make_async_copy(dmb_s, block_out, store_sem.at[1])
        a.start()
        b.start()
        step = 0
        pending = None
        while 15 + step <= red.last_tick() or step <= len(names):
            if pending is not None:
                pending.wait()
                gain_s[step] = gain_s[step - 1] + gain_s[len(names) + step]
                pending = None
            if step < len(names):
                pending = remote(gain_s.at[step], gain_s.at[len(names) + 1 + step], gsend_sem.at[step], grecv_sem.at[step],
                                 ids[names[step]])
                pending.start()
            red.tick(15 + step)
            step += 1
        gain_out[...] = pltpu.roll(gain_s[len(names)], width - fs * rows, 1)
        a.wait()
        b.wait()

    pairs = width // 128
    pl.run_scoped(attention, V((pairs, count, 128), bf16), V((pairs, count, 128), bf16), V((pairs, count, 128), bf16),
                  V((128, count), bf16), V((count, width), bf16), V((width, count), bf16), V((pairs, count, 128), bf16),
                  V((pairs, 8, count), f32),
                  V((count, width), bf16), V((18, count, 128), bf16), V((width, count), bf16), V((count, count), f32),
                  V((128, count), f32))
    for n in range(CHUNKS):
        red.store(n).wait()


def backward(reps, lengths, gain, tokens, cotangent, mid, q, k, v, a, at, h1t, log, cosine, sine, wq, wo, wf, wd):
    count, width = tokens.shape
    S = jax.ShapeDtypeStruct
    V = pltpu.VMEM
    dma = pltpu.SemaphoreType.DMA
    bits = reps.bit_length() - 1
    steps = 2 + bits
    exchanges = 10 + bits - 3
    lags = stage_lags(reps)
    shapes = [(2, 8), (8,), (4,), (3,)] + [(1,)] * (bits - 3)
    slots = [V((2 * lags[k],) + shape + (PIECE, 128), bf16) for k, shape in enumerate(shapes)]
    return pl.pallas_call(
        functools.partial(backward_kernel, reps),
        name="backward_reduce",
        in_specs=[SM, VM] + [ANY] * 16,
        out_specs=[ANY] * 3 + [VM],
        out_shape=[S((count, width), bf16), S((count, width), f32), S((CHUNKS, 8, PIECE, 128), bf16), S((8, width), f32)],
        scratch_shapes=[
            V((count, width), f32), V((count, width), f32), V((count, width), bf16), V((count, width), bf16),
            V((count, 128), f32), V((count, 128), f32), V((18, width, 128), bf16), V((6, width, 128), bf16),
            V((count, width), f32),
            V((SLOTS, 2, 2, 8, PIECE, 128), bf16), V((CHUNKS, 8, PIECE, 128), bf16), V((2 * steps + 1, 8, width), f32),
            dma((exchanges, 2 * max(lags))), dma((exchanges, 2 * max(lags))), dma((steps,)), dma((steps,)), dma((CHUNKS,)), dma((15,)), dma((2,))] + slots,
        compiler_params=pltpu.CompilerParams(collective_id=1, has_side_effects=True, vmem_limit_bytes=62 * 2**20),
    )(lengths, gain, tokens, cotangent, mid, q, k, v, a, at, h1t, log, cosine, sine, wq, wo, wf, wd)


def adamw(weight, first, second, grad, rate):
    first_new = beta_first * first + (1.0 - beta_first) * grad
    second_new = beta_second * second + (1.0 - beta_second) * grad * grad
    first_hat = first_new * (1.0 / (1.0 - beta_first**STEP))
    second_hat = second_new * (1.0 / (1.0 - beta_second**STEP))
    return (
        first_new,
        second_new,
        weight - rate * (first_hat / (jnp.sqrt(second_hat) + adam_eps) + decay_rate * weight),
    )


def update_tasks(width):
    rows = width // 4
    tasks = []
    for t in range(3):
        cols = [[(9 + c, r + 4 * ((2 * t + i) // 3), 48 * ((2 * t + i) % 3), 48) for r in range(4)]
                for c in range(3) for i in range(2)]
        tasks.append((0, (0, rows), t * width, cols))
    for k in range(8):
        tasks.append((2, (0, rows), 512 * k, [[(2 * j, k, 96, 48), (2 * j + 1, k, 0, 144)] for j in range(4)]))
    for j in range(4):
        tasks.append((3, (128 * j, 128), 0, [[(2 * j, k, 16 * c, 16) for k in range(8)] for c in range(6)]))
    tasks.append((1, (0, rows), 0, [[(8, r + 4 * (b // 3), 48 * (b % 3), 48) for r in range(4)] for b in range(6)]))
    return tasks


def update_kernel(rates, tasks, depth, grad_ref, gain_grad, *refs):
    state, refs = refs[:12], refs[12:]
    gain_state, refs = refs[:3], refs[3:]
    new, refs = refs[:12], refs[12:]
    gain_new, refs = refs[:3], refs[3:]
    taken, made, in_sem, out_sem = refs

    def moves(n, out):
        w, (row, rows), col, cols = tasks[n]
        wide = 128 * len(cols)
        slot = n % depth
        found = []
        for i in range(3):
            if out:
                found.append(pltpu.make_async_copy(made.at[slot, i, pl.ds(0, rows), pl.ds(0, wide)],
                                                   new[3 * w + i].at[pl.ds(row, rows), pl.ds(col, wide)], out_sem.at[slot, i]))
            else:
                found.append(pltpu.make_async_copy(state[3 * w + i].at[pl.ds(row, rows), pl.ds(col, wide)],
                                                   taken.at[slot, i, pl.ds(0, rows), pl.ds(0, wide)], in_sem.at[slot, i]))
        return found

    for n in range(depth):
        for c in moves(n, False):
            c.start()
    columns = gain_grad[0:2, 0:gain_new[0].shape[1]]
    for ref, value in zip((gain_new[1], gain_new[2], gain_new[0]), adamw(gain_state[0][...], gain_state[1][...], gain_state[2][...], columns, 1.0)):
        ref[...] = value
    for n, (w, (_, rows), _, cols) in enumerate(tasks):
        slot = n % depth
        for c in moves(n, False):
            c.wait()
        if n >= depth:
            for c in moves(n - depth, True):
                c.wait()
        for i, pieces in enumerate(cols):
            grad = jnp.concatenate([grad_ref[c, p, r:r + m, :] for c, p, r, m in pieces], axis=0).astype(f32)
            lanes = slice(128 * i, 128 * i + 128)
            held = [taken[slot, s, 0:rows, lanes] for s in range(3)]
            for s, value in zip((1, 2, 0), adamw(held[0], held[1], held[2], grad, rates[w])):
                made[slot, s, 0:rows, lanes] = value
        for c in moves(n, True):
            c.start()
        if n + depth < len(tasks):
            for c in moves(n + depth, False):
                c.start()
    for n in range(len(tasks) - depth, len(tasks)):
        for c in moves(n, True):
            c.wait()


def update(rates, grads, gain_grad, state, gain_state):
    width = gain_grad.shape[1]
    S = jax.ShapeDtypeStruct
    depth = 3
    dma = pltpu.SemaphoreType.DMA
    return pl.pallas_call(
        functools.partial(update_kernel, rates, update_tasks(width), depth),
        name="update",
        in_specs=[VM, VM] + [ANY] * 12 + [VM] * 3,
        out_specs=[ANY] * 12 + [VM] * 3,
        out_shape=[S(z.shape, f32) for z in state + gain_state],
        scratch_shapes=[pltpu.VMEM((depth, 3, width // 4, width), f32), pltpu.VMEM((depth, 3, width // 4, width), f32),
                        dma((depth, 3)), dma((depth, 3))],
        compiler_params=pltpu.CompilerParams(vmem_limit_bytes=60 * 2**20),
    )(grads, gain_grad, *state, *gain_state)


def shards(reps, tokens, cotangent, lengths, w_qkv, m_qkv, v_qkv, w_proj, m_proj, v_proj, w_ffn, m_ffn, v_ffn,
           w_down, m_down, v_down, gains, m_gains, v_gains):
    count, width = tokens.shape
    wq, wo, wf, wd, q, k, v, a, at, h1t, log, mid, gain, cosine, sine = forward(
        reps, lengths, tokens, gains, w_qkv, w_proj, w_ffn, w_down)
    block_out, input_grad, grads, gain_grad = backward(
        reps, lengths, gain, tokens, cotangent, mid, q, k, v, a, at, h1t, log, cosine, sine, wq, wo, wf, wd)
    wide = 3.0 * width ** (-0.5)
    proj = 3.0 * (count / (10.0 * width)) ** 0.5
    down = 6.0 * FF ** (-0.5)
    new = update(
        (wide, proj, wide, down), grads, gain_grad,
        (w_qkv, m_qkv, v_qkv, w_proj, m_proj, v_proj, w_ffn, m_ffn, v_ffn, w_down, m_down, v_down),
        (gains, m_gains, v_gains))
    return (block_out, input_grad) + tuple(new[3 * w + s] for w in range(5) for s in (1, 2, 0))


def solution(mesh):
    reps = mesh.shape["rep"]
    tokens = P(("rep", "fsdp"), None)
    weight = P("fsdp", None)
    gain = P(None, "fsdp")
    return jax.shard_map(
        functools.partial(shards, reps),
        mesh=mesh,
        in_specs=(tokens,) * 3 + (weight,) * 12 + (gain,) * 3,
        out_specs=(tokens,) * 2 + (weight,) * 12 + (gain,) * 3,
        check_vma=False,
    )
```

```python
import functools

import jax
import jax.numpy as jnp
import numpy as np
from jax import lax
from jax.experimental import pallas as pl
from jax.experimental.pallas import tpu as pltpu
from jax.sharding import PartitionSpec as P

HEADS = 12
FF = 2048
STEP = 10
norm_eps = 1e-05
rope_base = 10000.0
beta_first = 0.9
beta_second = 0.95
adam_eps = 1e-08
decay_rate = 0.1
LOG2E = 1.4426950408889634
MASKED = -1e30
MESH = pl.DeviceIdType.MESH
f32 = jnp.float32
bf16 = jnp.bfloat16
BLK = 256
CHUNKS = 12
PIECE = 144
SLOTS = 9
LAGS = (2, 2, 3, 3, 3)
ANY = pl.BlockSpec(memory_space=pl.ANY)
VM = pl.BlockSpec(memory_space=pltpu.VMEM)
SM = pl.BlockSpec(memory_space=pltpu.SMEM)


def dot(a, b, ca, cb):
    return lax.dot_general(a, b, (((ca,), (cb,)), ((), ())), preferred_element_type=f32)


def joined(ref, first, number):
    return jnp.concatenate([ref[first + i] for i in range(number)], axis=1)


def rows_of(i):
    return pl.ds(pl.multiple_of(i * BLK, BLK), BLK)


def lane_head(h, shape):
    return (lax.broadcasted_iota(jnp.int32, shape, 1) // 64) == h


def seq_ends(len_ref):
    total = 0
    ends = []
    for j in range(4):
        total = total + len_ref[0, j]
        ends.append(total)
    return ends


def fill_bias(ends, bias, count):
    q = lax.broadcasted_iota(jnp.int32, (1, count), 1)
    sq = sum((q >= e).astype(jnp.int32) for e in ends)

    @pl.loop(0, count // BLK)
    def _(j):
        k = lax.broadcasted_iota(jnp.int32, (BLK, 1), 0) + j * BLK
        sk = sum((k >= e).astype(jnp.int32) for e in ends)
        bias[rows_of(j), :] = jnp.where((sk == sq) & (k <= q), 0.0, MASKED)


def rope(block, cosine, sine, sign):
    lane = lax.broadcasted_iota(jnp.int32, block.shape, 1)
    swapped = jnp.where(lane % 64 < 32, pltpu.roll(block, 96, 1), pltpu.roll(block, 32, 1))
    if sign > 0:
        return block * cosine + swapped * sine
    return block * cosine - swapped * sine


def remote(src, dst, send_sem, recv_sem, device):
    return pltpu.make_async_remote_copy(
        src_ref=src, dst_ref=dst, send_sem=send_sem, recv_sem=recv_sem,
        device_id=device, device_id_type=MESH)


def unit_rows(value):
    inverse = lax.rsqrt(jnp.mean(value * value, axis=-1, keepdims=True) + norm_eps)
    return value * inverse, inverse


class Gather:
    def __init__(self, own, full, first, blocks, shard_rows, sems, index, ids, direct=False):
        self.direct = direct
        self.own, self.full, self.first, self.blocks, self.n = own, full, first, blocks, shard_rows
        self.ssem, self.rsem, self.w, self.ids = sems[0], sems[1], index, ids
        rep, fs = ids["rep"], ids["fsdp"]
        self.b0, self.b1 = rep % 2, (rep // 2) % 2
        self.q = rep % 4
        self.far = (fs + 2) % 4
        self.fs = fs
        self.quarter = shard_rows // 4

    def part(self, shard, quarter, quarters, half=None):
        row = pl.multiple_of(shard * self.n + quarter * self.quarter, 16)
        first, blocks = self.first, self.blocks
        if half is not None:
            blocks = blocks // 2
            first = first + half * blocks
        return self.full.at[pl.ds(first, blocks), pl.ds(row, quarters * self.quarter), :]

    def cp(self, i, ref, device, src=None):
        return remote(ref if src is None else src, ref, self.ssem.at[self.w, i], self.rsem.at[self.w, i], device)

    def copy(self, i):
        d = self.ids
        p, far, fs, q = self.part, self.far, self.fs, self.q
        q1 = (1 - self.b0) + 2 * self.b1
        q2 = self.b0 + 2 * (1 - self.b1)
        q3 = (1 - self.b0) + 2 * (1 - self.b1)
        own = own_quarter = None
        if self.own is not None:
            own = self.own.at[pl.ds(self.first, self.blocks)]
            own_quarter = self.own.at[pl.ds(self.first, self.blocks), pl.ds(pl.multiple_of(q * self.quarter, 16), self.quarter), :]
        if self.direct and i:
            return self.cp(i, p(fs if i == 1 else far, 0, 4), d["y" if i == 1 else "core"])
        return [
            lambda: self.cp(0, p(fs, 0, 4), d["core"], own),
            lambda: self.cp(1, p(fs, q, 1), d["y"], own_quarter),
            lambda: self.cp(2, p(far, q, 1, 0), d["bit0"]),
            lambda: self.cp(3, p(far, q, 1, 1), d["bit1"]),
            lambda: self.cp(4, p(far, q, 1), d["core"]),
            lambda: self.cp(5, p(far, 2 * self.b1, 2, 0), d["bit1"]),
            lambda: self.cp(6, p(far, q, 1, 1), d["bit0"]),
            lambda: self.cp(7, p(far, q2, 1, 1), d["bit0"]),
            lambda: self.cp(8, p(far, q1, 1, 0), d["core"]),
            lambda: self.cp(9, p(far, q2, 1, 1), d["core"]),
            lambda: self.cp(10, p(far, 2 * (1 - self.b1), 2, 0), d["core"]),
            lambda: self.cp(11, p(far, q1, 1, 1), d["core"]),
            lambda: self.cp(12, p(far, q3, 1, 1), d["core"]),
        ][i]()

    def step(self, waits, starts):
        for i in waits:
            self.copy(i).wait_recv()
        for i in starts:
            self.copy(i).start()

    def start(self):
        self.step((), (1, 0))

    def second(self):
        self.step((1,), (4,) if self.direct else (2, 3, 4))

    def third(self):
        self.step((2, 3), (5, 6, 7, 8, 9))

    def fourth(self):
        self.step((5, 6, 7), (10, 11, 12))

    def arrive(self):
        self.step((0, 4) if self.direct else (0, 4, 8, 9, 10, 11, 12), ())

    def sent(self):
        for i in (0, 1, 4) if self.direct else range(13):
            self.copy(i).wait_send()


def partners(rep, fs, reps):
    found = {"rep": rep, "fsdp": fs, "core": (rep, fs ^ 1), "y": (rep, fs ^ 2)}
    for b in range(reps.bit_length() - 1):
        found["bit%d" % b] = (rep ^ (1 << b), fs)
    for d in (1, 2, 3):
        found["z%d" % d] = (rep ^ (2 * (d // 2) + 4 * (d % 2)), fs)
    return found


def meet(ids, names):
    barrier = pltpu.get_barrier_semaphore()
    for name in names:
        pl.semaphore_signal(barrier, inc=1, device_id=ids[name], device_id_type=MESH)
    pl.semaphore_wait(barrier, len(names))


def place_gains(ref, rows, fs):
    ref[...] = pltpu.roll(ref[...], fs * rows, 1)


def forward_kernel(reps, len_ref, x_in, gain_in, freq_ref, wq_in, wo_in, wf_in, wd_in,
                   wq_out, wo_out, wf_out, wd_out, q_out, k_out, v_out, a_out, at_out, h1t_out, log_out, mid_out, gain_out, cos_out, sin_out,
                   wq_s, wo_s, st_q, st_o, st_f, st_d, own_f, own_d, gain_a, gain_b, gain_c, x_s, cos_s, sin_s,
                   h1_s, h1t_s, q_s, k_s, vt_s, v_s, a_s, at_s, log_s, mid_s, bias,
                   load_sem, store_sem, send_sem, recv_sem, gsend_sem, grecv_sem):
    count, width = x_s.shape
    pairs = width // 128
    rows = width // 4
    rep, fs = lax.axis_index("rep"), lax.axis_index("fsdp")
    ids = partners(rep, fs, reps)
    load_q = pltpu.make_async_copy(wq_in, st_q, load_sem.at[0])
    load_x = pltpu.make_async_copy(x_in, x_s, load_sem.at[1])
    load_o = pltpu.make_async_copy(wo_in, st_o, load_sem.at[2])
    load_f = pltpu.make_async_copy(wf_in, st_f, load_sem.at[3])
    load_d = pltpu.make_async_copy(wd_in, st_d, load_sem.at[4])
    for c in (load_q, load_x, load_o, load_f, load_d):
        c.start()
    gain_a[...] = jnp.zeros_like(gain_a)
    gain_a[0:2, 0:rows] = gain_in[...].astype(bf16).astype(f32)
    gain_a[...] = pltpu.roll(gain_a[...], fs * rows, 1)
    meet(ids, ("core", "y", "bit0", "bit1"))

    sems = (send_sem, recv_sem)
    near = [Gather(None, wq_s, 6 * c, 6, rows, sems, c, ids, c == 0) for c in range(3)]
    proj = Gather(None, wo_s, 0, 6, rows, sems, 3, ids)
    wide = [Gather(own_f, wf_out, 8 * j, 8, rows, sems, 4 + j, ids) for j in range(4)]
    down = Gather(own_d, wd_out, 0, 4, FF // 16, sems, 8, ids)

    g_core = remote(gain_a, gain_b, gsend_sem.at[0], grecv_sem.at[0], ids["core"])
    g_core.start()
    own_rows = pl.ds(pl.multiple_of(fs * rows, 16), rows)
    load_q.wait()
    for c in range(3):
        for t in range(3):
            for i in range(2):
                col = t * width + (2 * c + i) * 128
                wq_s[6 * c + 2 * t + i, own_rows, :] = st_q[:, col:col + 128].astype(bf16)
        if c < 2:
            near[c].start()
    load_o.wait()
    load_f.wait()
    for j in range(4):
        for n in range(8):
            col = (4 * n + j) * 128
            own_f[8 * j + n] = st_f[:, col:col + 128].astype(bf16)
    for i in range(6):
        wo_s[i, own_rows, :] = st_o[:, 128 * i:128 * i + 128].astype(bf16)
    load_d.wait()
    for j in range(4):
        own_d[j] = st_d[128 * j:128 * j + 128, :].astype(bf16)
    g_core.wait()
    gain_c[0] = gain_a[...] + gain_b[...]
    g_y = remote(gain_c.at[0], gain_c.at[1], gsend_sem.at[1], grecv_sem.at[1], ids["y"])
    g_y.start()
    near[1].second()
    near[2].start()
    wide[0].start()
    stores = [
        pltpu.make_async_copy(own_f, wf_out.at[:, own_rows, :], store_sem.at[0]),
        pltpu.make_async_copy(own_d, wd_out.at[:, pl.ds(pl.multiple_of(fs * (FF // 16), 16), FF // 16), :], store_sem.at[1]),
    ]
    for c in stores:
        c.start()
    ends = seq_ends(len_ref)
    token = lax.broadcasted_iota(jnp.int32, (1, count), 1)
    start = jnp.zeros((1, count), jnp.int32)
    for e in ends:
        start = jnp.where(token >= e, e, start)
    angle = freq_ref[:, 0:1] * (token - start).astype(f32)
    cosine, sine = jnp.cos(angle), jnp.sin(angle)
    cos_s[...] = jnp.concatenate([cosine] * 4, axis=0).T
    sin_s[...] = jnp.concatenate([-sine, sine, -sine, sine], axis=0).T
    near[2].second()
    wide[1].start()
    proj.start()
    near[1].third()
    g_y.wait()
    gain_out[...] = gain_c[0] + gain_c[1]
    g1 = gain_out[0:1, :]
    load_x.wait()

    @pl.loop(0, count // BLK)
    def _(i):
        blk = pl.ds(pl.multiple_of(i * BLK, BLK), BLK)
        x = x_s[blk, :].astype(f32)
        inverse = lax.rsqrt(jnp.mean(x * x, axis=-1, keepdims=True) + norm_eps)
        h1_s[blk, :] = (x * inverse * g1).astype(bf16)

    near[0].second()
    wide[0].second()
    wide[2].start()
    near[2].third()
    fill_bias(ends, bias, count)
    near[1].fourth()
    wide[3].start()

    def project(c):
        h1 = h1_s[...]
        for t in range(3):
            block = dot(h1, joined(wq_s, 6 * c + 2 * t, 2), 1, 0)
            for i in range(2):
                p = 2 * c + i
                piece = block[:, 128 * i:128 * i + 128]
                if t == 0:
                    q_s[p] = (rope(piece, cos_s[...], sin_s[...], 1) * (LOG2E / 8)).astype(bf16)
                elif t == 1:
                    k_s[p] = rope(piece, cos_s[...], sin_s[...], 1).astype(bf16)
                else:
                    v_s[p] = piece.astype(bf16)
                    vt_s[p] = piece.T.astype(bf16)

    def scores(p, i, h):
        q = q_s[p, i * BLK:(i + 1) * BLK, :]
        return dot(k_s[p, :BLK * (i + 1), :], jnp.where(lane_head(h, q.shape), q, 0), 1, 1)

    def soft(p, i, h, s):
        s = s + bias[:BLK * (i + 1), i * BLK:(i + 1) * BLK]
        largest = jnp.max(s, axis=0, keepdims=True)
        e = jnp.exp2(s - largest)
        total = jnp.sum(e, axis=0, keepdims=True)
        log_s[p, h:h + 1, i * BLK:(i + 1) * BLK] = largest + jnp.log2(total)
        return e.astype(bf16), total

    def mix(p, i, h, e, total):
        return dot(vt_s[p, 64 * h:64 * h + 64, :BLK * (i + 1)], e, 1, 0) * (1.0 / total)

    def attend(p):
        tasks = [(i, h) for i in range(count // BLK) for h in range(2)]
        s = scores(p, *tasks[0])
        held = None
        outs = {}
        for n, task in enumerate(tasks):
            ahead = scores(p, *tasks[n + 1]) if n + 1 < len(tasks) else None
            weighted = soft(p, *task, s)
            if held is not None:
                outs[held[0]] = mix(p, *held[0], *held[1])
            held = (task, weighted)
            s = ahead
        outs[held[0]] = mix(p, *held[0], *held[1])
        cols = pl.ds(pl.multiple_of(p * 128, 128), 128)
        for i in range(count // BLK):
            both = jnp.concatenate([outs[i, 0], outs[i, 1]], axis=0)
            at_s[cols, i * BLK:(i + 1) * BLK] = both.astype(bf16)
            a_s[i * BLK:(i + 1) * BLK, cols] = both.T.astype(bf16)

    ready = [pltpu.make_async_copy(src, dst, store_sem.at[3 + i]) for i, (src, dst) in enumerate((
        (wq_s, wq_out), (q_s, q_out), (k_s, k_out), (v_s, v_out), (cos_s, cos_out), (sin_s, sin_out)))]
    arrivals = [[near[0].arrive], [near[1].arrive], [near[2].arrive]]
    projected = [
        [near[2].fourth, wide[1].second, wide[0].third, down.start],
        [down.second, proj.third],
        [c.start for c in ready],
    ]
    attended = [
        [wide[1].third, wide[2].second, proj.second],
        [wide[0].fourth, wide[3].second, wide[2].third],
        [wide[1].fourth, wide[3].third],
        [wide[2].fourth, down.third, proj.fourth],
        [wide[3].fourth],
        [down.fourth],
    ]

    def at_turn(c, lists):
        for turn, steps in enumerate(lists):
            if steps:
                @pl.when(c == turn)
                def _():
                    for step in steps:
                        step()

    @pl.loop(0, 3)
    def _(c):
        at_turn(c, arrivals)
        project(c)
        at_turn(c, projected)

        @pl.loop(2 * c, 2 * c + 2)
        def _(p):
            attend(p)
            at_turn(p, attended)
    stores += ready
    proj.arrive()
    for i, (src, dst) in enumerate(((wo_s, wo_out), (a_s, a_out), (at_s, at_out), (log_s, log_out))):
        c = pltpu.make_async_copy(src, dst, store_sem.at[10 + i])
        c.start()
        stores.append(c)

    @pl.loop(0, count // BLK)
    def _(i):
        blk = pl.ds(pl.multiple_of(i * BLK, BLK), BLK)
        mid_s[blk, :] = x_s[blk, :].astype(f32) + dot(a_s[blk, :], joined(wo_s, 0, 6), 1, 0)
    c = pltpu.make_async_copy(mid_s, mid_out, store_sem.at[14])
    c.start()
    stores.append(c)

    @pl.loop(0, count // BLK)
    def _(i):
        blk = pl.ds(pl.multiple_of(i * BLK, BLK), BLK)
        h1t_s[:, blk] = h1_s[blk, :].astype(f32).T.astype(bf16)
    c = pltpu.make_async_copy(h1t_s, h1t_out, store_sem.at[9])
    c.start()
    stores.append(c)
    for g in wide + [down]:
        g.arrive()
    for g in near + [proj] + wide + [down]:
        g.sent()
    for c in stores:
        c.wait()


def frequencies():
    half = 32
    frequency = rope_base ** (-2.0 * np.arange(half) / (2 * half))
    return jnp.asarray(np.broadcast_to(frequency[:, None], (half, 128)), f32)


def forward(reps, lengths, tokens, gains, w_qkv, w_proj, w_ffn, w_down):
    count, width = tokens.shape
    pairs = width // 128
    S = jax.ShapeDtypeStruct
    V = pltpu.VMEM
    rows = width // 4
    dma = pltpu.SemaphoreType.DMA
    return pl.pallas_call(
        functools.partial(forward_kernel, reps),
        name="gather_forward",
        in_specs=[SM, ANY, VM, VM, ANY, ANY, ANY, ANY],
        out_specs=[ANY] * 12 + [VM] + [ANY] * 2,
        out_shape=[S((18, width, 128), bf16), S((6, width, 128), bf16), S((32, width, 128), bf16), S((4, FF // 4, width), bf16),
                   S((pairs, count, 128), bf16), S((pairs, count, 128), bf16), S((pairs, count, 128), bf16),
                   S((count, width), bf16), S((width, count), bf16), S((width, count), bf16), S((pairs, 8, count), f32),
                   S((count, width), f32), S((8, width), f32),
                   S((count, 128), f32), S((count, 128), f32)],
        scratch_shapes=[
            V((18, width, 128), bf16), V((6, width, 128), bf16), V((rows, 3 * width), f32), V((rows, width), f32),
            V((rows, 2 * FF), f32), V((FF // 4, width), f32), V((32, rows, 128), bf16), V((4, FF // 16, width), bf16),
            V((8, width), f32), V((8, width), f32), V((2, 8, width), f32),
            V((count, width), bf16), V((count, 128), f32), V((count, 128), f32),
            V((count, width), bf16), V((width, count), bf16), V((pairs, count, 128), bf16), V((pairs, count, 128), bf16),
            V((pairs, 128, count), bf16), V((pairs, count, 128), bf16), V((count, width), bf16), V((width, count), bf16),
            V((pairs, 8, count), f32), V((count, width), f32), V((count, count), f32),
            dma((5,)), dma((15,)), dma((9, 13)), dma((9, 13)), dma((2,)), dma((2,))],
        compiler_params=pltpu.CompilerParams(collective_id=0, has_side_effects=True, vmem_limit_bytes=60 * 2**20),
    )(lengths, tokens, gains, frequencies(), w_qkv, w_proj, w_ffn, w_down)


class Reduce:
    def __init__(self, ids, reps, grad, slots, kept, out, sems, out_sem):
        self.ids = ids
        self.grad, self.slots, self.kept, self.out = grad, slots, kept, out
        self.ssem, self.rsem = sems
        self.out_sem = out_sem
        rep, fs = ids["rep"], ids["fsdp"]
        self.core, self.y = fs % 2, fs // 2
        self.half = rep % 2
        self.z = 2 * (rep // 2 % 2) + rep // 4 % 2
        self.extra = reps.bit_length() - 1 - 3
        self.stages = 7 + self.extra
        self.offsets = stage_offsets(reps)
        self.lags = stage_lags(reps)

    def cp(self, kind, par, src, dst, device):
        return remote(src, dst, self.ssem.at[kind, par], self.rsem.at[kind, par], self.ids[device])

    def exchange(self, k, n):
        g = self.grad.at[n % SLOTS]
        mine = g.at[self.core, self.y]
        keep = self.kept.at[n]
        par = n % (2 * self.lags[k])
        first = 4 * self.half
        own = keep.at[pl.ds(first + self.z, 1)]
        if k == 0:
            return [self.cp(0, par, g.at[1 - self.core], self.slots[0].at[par], "core")]
        if k == 1:
            return [self.cp(1, par, g.at[self.core, 1 - self.y], self.slots[1].at[par], "y")]
        if k == 2:
            return [self.cp(2, par, mine.at[pl.ds(4 - first, 4)], self.slots[2].at[par], "bit0")]
        if k == 3:
            return [self.cp(2 + d, par, mine.at[first + (self.z ^ d)], self.slots[3].at[par, d - 1], "z%d" % d) for d in (1, 2, 3)]
        if k < 4 + self.extra:
            return [self.cp(6 + k, par, own, self.slots[k].at[par], "bit%d" % (k - 1))]
        if k == 4 + self.extra:
            return [self.cp(5 + d, par, own, own, "z%d" % d) for d in (1, 2, 3)]
        part = keep.at[pl.ds(first, 4)]
        return [self.cp(9, par, part, part, "bit0")]

    def start(self, k, n):
        for c in self.exchange(k, n):
            c.start()

    def add(self, n, first, number, slot, offset):
        mine = self.grad.at[n % SLOTS, self.core, self.y]

        @pl.loop(0, number)
        def _(i):
            mine[first + i] = (mine[first + i].astype(f32) + slot[offset + i].astype(f32)).astype(bf16)

    def stage(self, k, n):
        par = n % (2 * self.lags[k - 1])
        first = 4 * self.half
        if k > 0:
            for c in self.exchange(k - 1, n):
                c.wait()
        if k == 0:
            self.start(0, n)
        elif k == 1:
            g, slot = self.grad.at[n % SLOTS, self.core], self.slots[0].at[par]
            for y in (1 - self.y, self.y):
                @pl.loop(0, 8)
                def _(i):
                    g[y, i] = (g[y, i].astype(f32) + slot[y, i].astype(f32)).astype(bf16)
                if y is not self.y:
                    self.start(1, n)
        elif k == 2:
            self.add(n, 4 - first, 4, self.slots[1].at[par], 4 - first)
            self.start(2, n)
            self.add(n, first, 4, self.slots[1].at[par], first)
        elif k == 3:
            self.add(n, first, 4, self.slots[2].at[par], 0)
            self.start(3, n)
        elif k == 4:
            own = first + self.z
            slot = self.slots[3].at[par]
            total = self.grad[n % SLOTS, self.core, self.y, own].astype(f32) + slot[0].astype(f32)
            self.kept[n, own] = (total + slot[1].astype(f32) + slot[2].astype(f32)).astype(bf16)
            self.start(4, n)
        elif k <= 4 + self.extra:
            own = first + self.z
            slot = self.slots[k - 1].at[par]
            self.kept[n, own] = (self.kept[n, own].astype(f32) + slot[0].astype(f32)).astype(bf16)
            self.start(k, n)
        elif k < self.stages - 1:
            self.start(k, n)
        else:
            self.store(n).start()

    def store(self, n):
        return pltpu.make_async_copy(self.kept.at[n], self.out.at[n], self.out_sem.at[n])

    def tick(self, time):
        for k in reversed(range(self.stages)):
            since = time - self.offsets[k]
            if isinstance(time, int):
                if since < 0 or (since > 8 and since % 2) or since > 2 * CHUNKS - 10:
                    continue
                self.stage(k, since if since <= 8 else (since + 8) // 2)
            else:
                late = (since + 8) // 2
                fits = jnp.logical_and(since >= 0, jnp.logical_or(since <= 8, jnp.logical_and(since == 2 * late - 8, late < CHUNKS)))

                @pl.when(fits)
                def _():
                    self.stage(k, jnp.where(since <= 8, since, late))

    def last_tick(self):
        return 2 * CHUNKS - 10 + self.offsets[-1]


def stage_offsets(reps):
    stages = 7 + reps.bit_length() - 1 - 3
    return [0] + [1 + sum(LAGS[i] if i < len(LAGS) else LAGS[-1] for i in range(k)) for k in range(stages - 1)]


def stage_lags(reps):
    offsets = stage_offsets(reps)
    return [b - a for a, b in zip(offsets, offsets[1:])]


def put_pieces(slot, value, block):
    for s in range(4):
        for i in range(2):
            half, c = divmod(block + i, 3)
            for r in range(4):
                row = 192 * s + 48 * r
                slot[s % 2, s // 2, r + 4 * half, 48 * c:48 * c + 48, :] = value[row:row + 48, 128 * i:128 * i + 128]


def backward_kernel(reps, len_ref, gain_ref, x_in, cot_in, mid_in, q_in, k_in, v_in, a_in, at_in, h1t_in, log_in, cos_in, sin_in,
                    wq_in, wo_in, wf_in, wd_in,
                    block_out, input_grad, grad_out, gain_out,
                    mid_s, dmid_s, dy_s, x_s, cos_s, sin_s, wq_s, wo_s, out_s,
                    grad_s, kept_s, gain_s, send_sem, recv_sem, gsend_sem, grecv_sem, out_sem, load_sem, store_sem, *slots):
    count, width = x_s.shape
    rows = width // 4
    blocks = count // BLK
    rep, fs = lax.axis_index("rep"), lax.axis_index("fsdp")
    ids = partners(rep, fs, reps)
    bits = reps.bit_length() - 1
    names = ("core", "y") + tuple("bit%d" % b for b in range(bits))
    friends = names[:3] + ("z1", "z2", "z3") + names[5:]
    red = Reduce(ids, reps, grad_s, slots, kept_s, grad_out, (send_sem, recv_sem), out_sem)
    ends = seq_ends(len_ref)
    valid = ends[3]

    def load(i, src, dst):
        c = pltpu.make_async_copy(src, dst, load_sem.at[i])
        c.start()
        return c

    g1, g2 = gain_ref[0:1, :], gain_ref[1:2, :]

    def feed(wf_s, wd_s, h2_s, h2t_s, z_s, df_s):
        need = [load(0, mid_in, mid_s), load(1, cot_in, dy_s)]
        def weights(j):
            return [pltpu.make_async_copy(wf_in.at[pl.ds(8 * j, 8)], wf_s.at[pl.ds(8 * j, 8)], load_sem.at[2 + 2 * j]),
                    pltpu.make_async_copy(wd_in.at[j], wd_s.at[j], load_sem.at[3 + 2 * j])]

        for j in range(4):
            for c in weights(j):
                c.start()
        late = [load(10, x_in, x_s), load(11, cos_in, cos_s), load(12, sin_in, sin_s), load(13, wq_in, wq_s),
                load(14, wo_in, wo_s)]
        meet(ids, friends)
        for c in need:
            c.wait()

        @pl.loop(0, blocks)
        def _(i):
            blk = rows_of(i)
            unit, _ = unit_rows(mid_s[blk, :])
            h2 = unit * g2
            h2_s[blk, :] = h2.astype(bf16)
            h2t_s[:, blk] = h2.T.astype(bf16)
            token = lax.broadcasted_iota(jnp.int32, (BLK, 1), 0) + i * BLK
            dy_s[blk, :] = jnp.where(token < valid, dy_s[blk, :], 0)
            out_s[blk, :] = mid_s[blk, :]
            dmid_s[blk, :] = jnp.zeros((BLK, width), f32)

        @pl.loop(0, 4)
        def _(j):
            for c in weights(j):
                c.wait()

            @pl.loop(0, blocks)
            def _(i):
                blk = rows_of(i)
                h2 = h2_s[blk, :]
                gate = dot(h2, joined(wf_s, 8 * j, 4), 1, 0)
                up = dot(h2, joined(wf_s, 8 * j + 4, 4), 1, 0)
                dz = dot(dy_s[blk, :], wd_s[j], 1, 1)
                sg = 1.0 / (1.0 + jnp.exp(-gate))
                silu = gate * sg
                z = (silu * up).astype(bf16)
                z_s[blk, :] = z
                dgate = (dz * up * (sg * (1.0 + gate * (1.0 - sg)))).astype(bf16)
                dup = (dz * silu).astype(bf16)
                df_s[blk, 0:512] = dgate
                df_s[blk, 512:1024] = dup
                out_s[blk, :] += dot(z, wd_s[j], 1, 0)
                dmid_s[blk, :] += dot(jnp.concatenate([dgate, dup], axis=1), joined(wf_s, 8 * j, 8), 1, 1)

            red.tick(2 * j - 1)
            gwd = dot(z_s[...], dy_s[...], 0, 0).astype(bf16)
            for s in range(4):
                for k in range(8):
                    for c in range(6):
                        row = 128 * s + 16 * k
                        grad_s[2 * j, s % 2, s // 2, k, 16 * c:16 * c + 16, :] = gwd[row:row + 16, 128 * c:128 * c + 128]

            @pl.loop(0, 4)
            def _(n):
                gwf = dot(h2t_s[...], df_s[:, pl.ds(pl.multiple_of(256 * n, 256), 256)], 1, 0).astype(bf16)
                for s in range(4):
                    for i in range(2):
                        lanes = slice(128 * i, 128 * i + 128)
                        grad_s[2 * j, s % 2, s // 2, 2 * n + i, 96:144, :] = gwf[rows * s:rows * s + 48, lanes]
                        grad_s[2 * j + 1, s % 2, s // 2, 2 * n + i, 0:144, :] = gwf[rows * s + 48:rows * s + rows, lanes]
            red.tick(2 * j)
        for c in late:
            c.wait()

    V = pltpu.VMEM
    pl.run_scoped(feed, V((32, width, 128), bf16), V((4, FF // 4, width), bf16), V((count, width), bf16),
                  V((width, count), bf16), V((count, 512), bf16), V((count, 1024), bf16))

    def attention(q_s, k_s, v_s, kt_s, a_s, at_s, da_s, log_s, dmb_s, dq3_s, h1t_s, bias, dqt_s):
        need = [load(0, q_in, q_s), load(1, k_in, k_s), load(2, v_in, v_s), load(3, log_in, log_s), load(4, a_in, a_s),
                load(5, at_in, at_s), load(6, h1t_in, h1t_s)]

        gain_s[...] = jnp.zeros_like(gain_s)
        @pl.loop(0, blocks)
        def _(i):
            blk = rows_of(i)
            unit, inverse = unit_rows(mid_s[blk, :])
            dh = dmid_s[blk, :]
            gain_s[0, 1:2, :] += jnp.sum(dh * unit, axis=0, keepdims=True)
            scaled = dh * g2
            dmid = dy_s[blk, :].astype(f32) + inverse * (scaled - unit * jnp.mean(scaled * unit, axis=-1, keepdims=True))
            dmid_s[blk, :] = dmid
            dmb_s[blk, :] = dmid.astype(bf16)
            mid_s[blk, :] = out_s[blk, :]
        red.tick(7)
        for c in need:
            c.wait()

        @pl.loop(0, 3)
        def _(c):
            part = pl.ds(pl.multiple_of(c * 256, 256), 256)
            weight = jnp.concatenate([wo_s[i, part, :] for i in range(6)], axis=1)
            da = dot(dmb_s[...], weight, 1, 1).astype(bf16)
            da_s[2 * c] = da[:, 0:128]
            da_s[2 * c + 1] = da[:, 128:256]
        for n in range(3):
            gwo = dot(at_s[...], dmb_s[:, 256 * n:256 * n + 256], 1, 0).astype(bf16)
            put_pieces(grad_s.at[8], gwo, 2 * n)
        red.tick(8)
        fill_bias(ends, bias, count)

        def pair(p, place):
            kt_s[...] = k_s[p].T
            cols = pl.ds(pl.multiple_of(p * 128, 128), 128)
            product = da_s[p].astype(f32) * a_s[:, cols].astype(f32)
            pick = ((lax.broadcasted_iota(jnp.int32, (8, 128), 1) // 64)
                    == lax.broadcasted_iota(jnp.int32, (8, 128), 0)).astype(bf16)
            high = product.astype(bf16)
            low = (product - high.astype(f32)).astype(bf16)
            centred = dot(pick, high, 1, 1) + dot(pick, low, 1, 1)

            def first(j, h):
                lo = j * BLK
                q, da = q_s[p, lo:, :], da_s[p, lo:, :]
                mine = lane_head(h, q.shape)
                q, da = jnp.where(mine, q, 0), jnp.where(mine, da, 0)
                return dot(k_s[p, lo:lo + BLK, :], q, 1, 1), dot(v_s[p, lo:lo + BLK, :], da, 1, 1), q, da

            def middle(j, h, s, dp):
                lo = j * BLK
                weight = jnp.exp2(s + bias[lo:lo + BLK, lo:] - log_s[p, h:h + 1, lo:])
                ds = (weight * (dp - centred[h:h + 1, lo:])).astype(bf16)
                return weight.astype(bf16), ds

            sums = {}

            def last(j, h, weight, ds, q, da):
                lo = j * BLK
                dv, dk = dot(weight, da, 1, 0), dot(ds, q, 1, 0)
                dq = dot(kt_s[64 * h:64 * h + 64, lo:lo + BLK], ds, 1, 0)
                if j == 0:
                    dqt_s[64 * h:64 * h + 64, :] = dq
                else:
                    dqt_s[64 * h:64 * h + 64, lo:] += dq
                if j in sums:
                    dk, dv = dk + sums[j][0], dv + sums[j][1]
                    dk = rope(dk * (1.0 / LOG2E), cos_s[lo:lo + BLK, :], sin_s[lo:lo + BLK, :], -1)
                    dq3_s[place + 2, lo:lo + BLK, :] = dk.astype(bf16)
                    dq3_s[place + 4, lo:lo + BLK, :] = dv.astype(bf16)
                else:
                    sums[j] = (dk, dv)

            tasks = [(j, h) for j in range(blocks) for h in range(2)]
            now = first(*tasks[0])
            held = None
            for n, task in enumerate(tasks):
                ahead = first(*tasks[n + 1]) if n + 1 < len(tasks) else None
                pd = middle(*task, now[0], now[1])
                if held is not None:
                    last(*held)
                held = (*task, *pd, now[2], now[3])
                now = ahead
            last(*held)
            dq3_s[place] = rope(dqt_s[...].T * 0.125, cos_s[...], sin_s[...], -1).astype(bf16)

        @pl.loop(0, 3)
        def _(c):
            @pl.loop(0, 2)
            def _(i):
                pair(2 * c + i, 6 * c + i)

                @pl.when(i == 0)
                def _():
                    red.tick(9 + 2 * c)
            for t in range(3):
                gwq = dot(h1t_s[...], joined(dq3_s, 6 * c + 2 * t, 2), 1, 0).astype(bf16)
                put_pieces(grad_s.at[c], gwq, 2 * t)
            red.tick(10 + 2 * c)

        @pl.loop(0, blocks)
        def _(i):
            blk = rows_of(i)
            dq3 = jnp.concatenate([dq3_s[n, blk, :] for n in range(18)], axis=1)
            dh = dot(dq3, joined(wq_s, 0, 18), 1, 1)
            unit, inverse = unit_rows(x_s[blk, :].astype(f32))
            gain_s[0, 0:1, :] += jnp.sum(dh * unit, axis=0, keepdims=True)
            scaled = dh * g1
            dmid_s[blk, :] += inverse * (scaled - unit * jnp.mean(scaled * unit, axis=-1, keepdims=True))
            dmb_s[blk, :] = mid_s[blk, :].astype(bf16)
            red.tick(15 + i)

        a = pltpu.make_async_copy(dmid_s, input_grad, store_sem.at[0])
        b = pltpu.make_async_copy(dmb_s, block_out, store_sem.at[1])
        a.start()
        b.start()
        step = 0
        pending = None
        drain = 15 + blocks
        while drain + step <= red.last_tick() or step <= len(names):
            if pending is not None:
                pending.wait()
                gain_s[step] = gain_s[step - 1] + gain_s[len(names) + step]
                pending = None
            if step < len(names):
                pending = remote(gain_s.at[step], gain_s.at[len(names) + 1 + step], gsend_sem.at[step], grecv_sem.at[step],
                                 ids[names[step]])
                pending.start()
            red.tick(drain + step)
            step += 1
        gain_out[...] = pltpu.roll(gain_s[len(names)], width - fs * rows, 1)
        a.wait()
        b.wait()

    pairs = width // 128
    pl.run_scoped(attention, V((pairs, count, 128), bf16), V((pairs, count, 128), bf16), V((pairs, count, 128), bf16),
                  V((128, count), bf16), V((count, width), bf16), V((width, count), bf16), V((pairs, count, 128), bf16),
                  V((pairs, 8, count), f32),
                  V((count, width), bf16), V((18, count, 128), bf16), V((width, count), bf16), V((count, count), f32),
                  V((128, count), f32))
    for n in range(CHUNKS):
        red.store(n).wait()


def backward(reps, lengths, gain, tokens, cotangent, mid, q, k, v, a, at, h1t, log, cosine, sine, wq, wo, wf, wd):
    count, width = tokens.shape
    S = jax.ShapeDtypeStruct
    V = pltpu.VMEM
    dma = pltpu.SemaphoreType.DMA
    bits = reps.bit_length() - 1
    steps = 2 + bits
    exchanges = 10 + bits - 3
    lags = stage_lags(reps)
    shapes = [(2, 8), (8,), (4,), (3,)] + [(1,)] * (bits - 3)
    slots = [V((2 * lags[k],) + shape + (PIECE, 128), bf16) for k, shape in enumerate(shapes)]
    return pl.pallas_call(
        functools.partial(backward_kernel, reps),
        name="backward_reduce",
        in_specs=[SM, VM] + [ANY] * 16,
        out_specs=[ANY] * 3 + [VM],
        out_shape=[S((count, width), bf16), S((count, width), f32), S((CHUNKS, 8, PIECE, 128), bf16), S((8, width), f32)],
        scratch_shapes=[
            V((count, width), f32), V((count, width), f32), V((count, width), bf16), V((count, width), bf16),
            V((count, 128), f32), V((count, 128), f32), V((18, width, 128), bf16), V((6, width, 128), bf16),
            V((count, width), f32),
            V((SLOTS, 2, 2, 8, PIECE, 128), bf16), V((CHUNKS, 8, PIECE, 128), bf16), V((2 * steps + 1, 8, width), f32),
            dma((exchanges, 2 * max(lags))), dma((exchanges, 2 * max(lags))), dma((steps,)), dma((steps,)), dma((CHUNKS,)), dma((15,)), dma((2,))] + slots,
        compiler_params=pltpu.CompilerParams(collective_id=1, has_side_effects=True, vmem_limit_bytes=62 * 2**20),
    )(lengths, gain, tokens, cotangent, mid, q, k, v, a, at, h1t, log, cosine, sine, wq, wo, wf, wd)


def adamw(weight, first, second, grad, rate):
    first_new = beta_first * first + (1.0 - beta_first) * grad
    second_new = beta_second * second + (1.0 - beta_second) * grad * grad
    first_hat = first_new * (1.0 / (1.0 - beta_first**STEP))
    second_hat = second_new * (1.0 / (1.0 - beta_second**STEP))
    return (
        first_new,
        second_new,
        weight - rate * (first_hat / (jnp.sqrt(second_hat) + adam_eps) + decay_rate * weight),
    )


def update_tasks(width):
    rows = width // 4
    tasks = []
    for t in range(3):
        cols = [[(9 + c, r + 4 * ((2 * t + i) // 3), 48 * ((2 * t + i) % 3), 48) for r in range(4)]
                for c in range(3) for i in range(2)]
        tasks.append((0, (0, rows), t * width, cols))
    for k in range(8):
        tasks.append((2, (0, rows), 512 * k, [[(2 * j, k, 96, 48), (2 * j + 1, k, 0, 144)] for j in range(4)]))
    for j in range(4):
        tasks.append((3, (128 * j, 128), 0, [[(2 * j, k, 16 * c, 16) for k in range(8)] for c in range(6)]))
    tasks.append((1, (0, rows), 0, [[(8, r + 4 * (b // 3), 48 * (b % 3), 48) for r in range(4)] for b in range(6)]))
    return tasks


def update_kernel(rates, tasks, depth, grad_ref, gain_grad, *refs):
    passed, refs = refs[:2], refs[2:]
    state, refs = refs[:12], refs[12:]
    gain_state, refs = refs[:3], refs[3:]
    new, refs = refs[:12], refs[12:]
    gain_new, refs = refs[:3], refs[3:]
    given, refs = refs[:2], refs[2:]
    taken, made, in_sem, out_sem, low_s, wide_s, pass_sem = refs
    holds = (low_s, wide_s)
    through = [pltpu.make_async_copy(passed[i], holds[i], pass_sem.at[i]) for i in range(2)]
    onward = [pltpu.make_async_copy(holds[i], given[i], pass_sem.at[2 + i]) for i in range(2)]

    def moves(n, out):
        w, (row, rows), col, cols = tasks[n]
        wide = 128 * len(cols)
        slot = n % depth
        found = []
        for i in range(3):
            if out:
                found.append(pltpu.make_async_copy(made.at[slot, i, pl.ds(0, rows), pl.ds(0, wide)],
                                                   new[3 * w + i].at[pl.ds(row, rows), pl.ds(col, wide)], out_sem.at[slot, i]))
            else:
                found.append(pltpu.make_async_copy(state[3 * w + i].at[pl.ds(row, rows), pl.ds(col, wide)],
                                                   taken.at[slot, i, pl.ds(0, rows), pl.ds(0, wide)], in_sem.at[slot, i]))
        return found

    for n in range(depth):
        for c in moves(n, False):
            c.start()
    columns = gain_grad[0:2, 0:gain_new[0].shape[1]]
    for ref, value in zip((gain_new[1], gain_new[2], gain_new[0]), adamw(gain_state[0][...], gain_state[1][...], gain_state[2][...], columns, 1.0)):
        ref[...] = value
    for n, (w, (_, rows), _, cols) in enumerate(tasks):
        slot = n % depth
        for c in moves(n, False):
            c.wait()
        if n >= depth:
            for c in moves(n - depth, True):
                c.wait()
        for i, pieces in enumerate(cols):
            grad = jnp.concatenate([grad_ref[c, p, r:r + m, :] for c, p, r, m in pieces], axis=0).astype(f32)
            lanes = slice(128 * i, 128 * i + 128)
            held = [taken[slot, s, 0:rows, lanes] for s in range(3)]
            for s, value in zip((1, 2, 0), adamw(held[0], held[1], held[2], grad, rates[w])):
                made[slot, s, 0:rows, lanes] = value
        for c in moves(n, True):
            c.start()
        if n + depth < len(tasks):
            for c in moves(n + depth, False):
                c.start()
        if n == 2:
            for c in through:
                c.start()
        if n == 8:
            for a, b in zip(through, onward):
                a.wait()
                b.start()
    for n in range(len(tasks) - depth, len(tasks)):
        for c in moves(n, True):
            c.wait()
    for c in onward:
        c.wait()


def update(rates, grads, gain_grad, through, state, gain_state):
    width = gain_grad.shape[1]
    S = jax.ShapeDtypeStruct
    depth = 6
    dma = pltpu.SemaphoreType.DMA
    return pl.pallas_call(
        functools.partial(update_kernel, rates, update_tasks(width), depth),
        name="update",
        in_specs=[VM, VM] + [ANY] * 14 + [VM] * 3,
        out_specs=[ANY] * 12 + [VM] * 3 + [ANY] * 2,
        out_shape=[S(z.shape, z.dtype) for z in state + gain_state + through],
        scratch_shapes=[pltpu.VMEM((depth, 3, width // 4, width), f32), pltpu.VMEM((depth, 3, width // 4, width), f32),
                        dma((depth, 3)), dma((depth, 3))]
        + [pltpu.VMEM(z.shape, z.dtype) for z in through] + [dma((4,))],
        compiler_params=pltpu.CompilerParams(vmem_limit_bytes=60 * 2**20),
    )(grads, gain_grad, *through, *state, *gain_state)


def shards(reps, tokens, cotangent, lengths, w_qkv, m_qkv, v_qkv, w_proj, m_proj, v_proj, w_ffn, m_ffn, v_ffn,
           w_down, m_down, v_down, gains, m_gains, v_gains):
    count, width = tokens.shape
    wq, wo, wf, wd, q, k, v, a, at, h1t, log, mid, gain, cosine, sine = forward(
        reps, lengths, tokens, gains, w_qkv, w_proj, w_ffn, w_down)
    block_out, input_grad, grads, gain_grad = backward(
        reps, lengths, gain, tokens, cotangent, mid, q, k, v, a, at, h1t, log, cosine, sine, wq, wo, wf, wd)
    wide = 3.0 * width ** (-0.5)
    proj = 3.0 * (count / (10.0 * width)) ** 0.5
    down = 6.0 * FF ** (-0.5)
    new = update(
        (wide, proj, wide, down), grads, gain_grad, (block_out, input_grad),
        (w_qkv, m_qkv, v_qkv, w_proj, m_proj, v_proj, w_ffn, m_ffn, v_ffn, w_down, m_down, v_down),
        (gains, m_gains, v_gains))
    return (new[15], new[16]) + tuple(new[3 * w + s] for w in range(5) for s in (1, 2, 0))


def solution(mesh):
    reps = mesh.shape["rep"]
    tokens = P(("rep", "fsdp"), None)
    weight = P("fsdp", None)
    gain = P(None, "fsdp")
    return jax.shard_map(
        functools.partial(shards, reps),
        mesh=mesh,
        in_specs=(tokens,) * 3 + (weight,) * 12 + (gain,) * 3,
        out_specs=(tokens,) * 2 + (weight,) * 12 + (gain,) * 3,
        check_vma=False,
    )
```

```python
import functools

import jax
import jax.numpy as jnp
import numpy as np
from jax import lax
from jax.experimental import pallas as pl
from jax.experimental.pallas import tpu as pltpu
from jax.sharding import PartitionSpec as P

HEADS = 12
FF = 2048
STEP = 10
norm_eps = 1e-05
rope_base = 10000.0
beta_first = 0.9
beta_second = 0.95
adam_eps = 1e-08
decay_rate = 0.1
LOG2E = 1.4426950408889634
MASKED = -1e30
MESH = pl.DeviceIdType.MESH
f32 = jnp.float32
bf16 = jnp.bfloat16
BLK = 256
CHUNKS = 12
PIECE = 144
SLOTS = 9
LAGS = (2, 2, 3, 3, 3)
ANY = pl.BlockSpec(memory_space=pl.ANY)
VM = pl.BlockSpec(memory_space=pltpu.VMEM)
SM = pl.BlockSpec(memory_space=pltpu.SMEM)


def dot(a, b, ca, cb):
    return lax.dot_general(a, b, (((ca,), (cb,)), ((), ())), preferred_element_type=f32)


def joined(ref, first, number):
    return jnp.concatenate([ref[first + i] for i in range(number)], axis=1)


def rows_of(i):
    return pl.ds(pl.multiple_of(i * BLK, BLK), BLK)


def lane_head(h, shape):
    return (lax.broadcasted_iota(jnp.int32, shape, 1) // 64) == h


def seq_ends(len_ref):
    total = 0
    ends = []
    for j in range(4):
        total = total + len_ref[0, j]
        ends.append(total)
    return ends


def fill_bias(ends, bias, count):
    q = lax.broadcasted_iota(jnp.int32, (1, count), 1)
    sq = sum((q >= e).astype(jnp.int32) for e in ends)

    @pl.loop(0, count // BLK)
    def _(j):
        k = lax.broadcasted_iota(jnp.int32, (BLK, 1), 0) + j * BLK
        sk = sum((k >= e).astype(jnp.int32) for e in ends)
        bias[rows_of(j), :] = jnp.where((sk == sq) & (k <= q), 0.0, MASKED)


def rope(block, cosine, sine, sign):
    lane = lax.broadcasted_iota(jnp.int32, block.shape, 1)
    swapped = jnp.where(lane % 64 < 32, pltpu.roll(block, 96, 1), pltpu.roll(block, 32, 1))
    if sign > 0:
        return block * cosine + swapped * sine
    return block * cosine - swapped * sine


def remote(src, dst, send_sem, recv_sem, device):
    return pltpu.make_async_remote_copy(
        src_ref=src, dst_ref=dst, send_sem=send_sem, recv_sem=recv_sem,
        device_id=device, device_id_type=MESH)


def unit_rows(value):
    inverse = lax.rsqrt(jnp.mean(value * value, axis=-1, keepdims=True) + norm_eps)
    return value * inverse, inverse


class Gather:
    def __init__(self, own, full, first, blocks, shard_rows, sems, index, ids, direct=False):
        self.direct = direct
        self.own, self.full, self.first, self.blocks, self.n = own, full, first, blocks, shard_rows
        self.ssem, self.rsem, self.w, self.ids = sems[0], sems[1], index, ids
        rep, fs = ids["rep"], ids["fsdp"]
        self.b0, self.b1 = rep % 2, (rep // 2) % 2
        self.q = rep % 4
        self.far = (fs + 2) % 4
        self.fs = fs
        self.quarter = shard_rows // 4

    def part(self, shard, quarter, quarters, half=None):
        row = pl.multiple_of(shard * self.n + quarter * self.quarter, 16)
        first, blocks = self.first, self.blocks
        if half is not None:
            blocks = blocks // 2
            first = first + half * blocks
        return self.full.at[pl.ds(first, blocks), pl.ds(row, quarters * self.quarter), :]

    def cp(self, i, ref, device, src=None):
        return remote(ref if src is None else src, ref, self.ssem.at[self.w, i], self.rsem.at[self.w, i], device)

    def copy(self, i):
        d = self.ids
        p, far, fs, q = self.part, self.far, self.fs, self.q
        q1 = (1 - self.b0) + 2 * self.b1
        q2 = self.b0 + 2 * (1 - self.b1)
        q3 = (1 - self.b0) + 2 * (1 - self.b1)
        own = own_quarter = None
        if self.own is not None:
            own = self.own.at[pl.ds(self.first, self.blocks)]
            own_quarter = self.own.at[pl.ds(self.first, self.blocks), pl.ds(pl.multiple_of(q * self.quarter, 16), self.quarter), :]
        if self.direct and i:
            return self.cp(i, p(fs if i == 1 else far, 0, 4), d["y" if i == 1 else "core"])
        return [
            lambda: self.cp(0, p(fs, 0, 4), d["core"], own),
            lambda: self.cp(1, p(fs, q, 1), d["y"], own_quarter),
            lambda: self.cp(2, p(far, q, 1, 0), d["bit0"]),
            lambda: self.cp(3, p(far, q, 1, 1), d["bit1"]),
            lambda: self.cp(4, p(far, q, 1), d["core"]),
            lambda: self.cp(5, p(far, 2 * self.b1, 2, 0), d["bit1"]),
            lambda: self.cp(6, p(far, q, 1, 1), d["bit0"]),
            lambda: self.cp(7, p(far, q2, 1, 1), d["bit0"]),
            lambda: self.cp(8, p(far, q1, 1, 0), d["core"]),
            lambda: self.cp(9, p(far, q2, 1, 1), d["core"]),
            lambda: self.cp(10, p(far, 2 * (1 - self.b1), 2, 0), d["core"]),
            lambda: self.cp(11, p(far, q1, 1, 1), d["core"]),
            lambda: self.cp(12, p(far, q3, 1, 1), d["core"]),
        ][i]()

    def step(self, waits, starts):
        for i in waits:
            self.copy(i).wait_recv()
        for i in starts:
            self.copy(i).start()

    def start(self):
        self.step((), (1, 0))

    def second(self):
        self.step((1,), (4,) if self.direct else (2, 3, 4))

    def third(self):
        self.step((2, 3), (5, 6, 7, 8, 9))

    def fourth(self):
        self.step((5, 6, 7), (10, 11, 12))

    def arrive(self):
        self.step((0, 4) if self.direct else (0, 4, 8, 9, 10, 11, 12), ())

    def sent(self):
        for i in (0, 1, 4) if self.direct else range(13):
            self.copy(i).wait_send()


def partners(rep, fs, reps):
    found = {"rep": rep, "fsdp": fs, "core": (rep, fs ^ 1), "y": (rep, fs ^ 2)}
    for b in range(reps.bit_length() - 1):
        found["bit%d" % b] = (rep ^ (1 << b), fs)
    for d in (1, 2, 3):
        found["z%d" % d] = (rep ^ (2 * (d // 2) + 4 * (d % 2)), fs)
    return found


def greet(ids, names):
    for name in names:
        pl.semaphore_signal(pltpu.get_barrier_semaphore(), inc=1, device_id=ids[name], device_id_type=MESH)


def meet(names):
    pl.semaphore_wait(pltpu.get_barrier_semaphore(), len(names))


def place_gains(ref, rows, fs):
    ref[...] = pltpu.roll(ref[...], fs * rows, 1)


def forward_kernel(reps, len_ref, x_in, gain_in, freq_ref, wq_in, wo_in, wf_in, wd_in,
                   wq_out, wo_out, wf_out, wd_out, q_out, k_out, v_out, a_out, at_out, h1t_out, log_out, mid_out, gain_out, cos_out, sin_out,
                   wq_s, wo_s, st_q, st_o, st_f, st_d, own_f, own_d, gain_a, gain_b, gain_c, x_s, cos_s, sin_s,
                   h1_s, h1t_s, q_s, k_s, vt_s, v_s, a_s, at_s, log_s, mid_s, bias,
                   load_sem, store_sem, send_sem, recv_sem, gsend_sem, grecv_sem):
    count, width = x_s.shape
    pairs = width // 128
    rows = width // 4
    rep, fs = lax.axis_index("rep"), lax.axis_index("fsdp")
    ids = partners(rep, fs, reps)
    load_q = pltpu.make_async_copy(wq_in, st_q, load_sem.at[0])
    load_x = pltpu.make_async_copy(x_in, x_s, load_sem.at[1])
    load_o = pltpu.make_async_copy(wo_in, st_o, load_sem.at[2])
    load_f = pltpu.make_async_copy(wf_in, st_f, load_sem.at[3])
    load_d = pltpu.make_async_copy(wd_in, st_d, load_sem.at[4])
    for c in (load_q, load_x, load_o, load_f, load_d):
        c.start()
    gain_a[...] = jnp.zeros_like(gain_a)
    gain_a[0:2, 0:rows] = gain_in[...].astype(bf16).astype(f32)
    gain_a[...] = pltpu.roll(gain_a[...], fs * rows, 1)
    friends = ("core", "y", "bit0", "bit1")
    greet(ids, friends)
    meet(friends)

    sems = (send_sem, recv_sem)
    near = [Gather(None, wq_s, 6 * c, 6, rows, sems, c, ids, c == 0) for c in range(3)]
    proj = Gather(None, wo_s, 0, 6, rows, sems, 3, ids)
    wide = [Gather(own_f, wf_out, 8 * j, 8, rows, sems, 4 + j, ids) for j in range(4)]
    down = Gather(own_d, wd_out, 0, 4, FF // 16, sems, 8, ids)

    g_core = remote(gain_a, gain_b, gsend_sem.at[0], grecv_sem.at[0], ids["core"])
    g_core.start()
    own_rows = pl.ds(pl.multiple_of(fs * rows, 16), rows)
    load_q.wait()
    for c in range(3):
        for t in range(3):
            for i in range(2):
                col = t * width + (2 * c + i) * 128
                wq_s[6 * c + 2 * t + i, own_rows, :] = st_q[:, col:col + 128].astype(bf16)
        if c < 2:
            near[c].start()
    load_o.wait()
    load_f.wait()
    for j in range(4):
        for n in range(8):
            col = (4 * n + j) * 128
            own_f[8 * j + n] = st_f[:, col:col + 128].astype(bf16)
    for i in range(6):
        wo_s[i, own_rows, :] = st_o[:, 128 * i:128 * i + 128].astype(bf16)
    load_d.wait()
    for j in range(4):
        own_d[j] = st_d[128 * j:128 * j + 128, :].astype(bf16)
    g_core.wait()
    gain_c[0] = gain_a[...] + gain_b[...]
    g_y = remote(gain_c.at[0], gain_c.at[1], gsend_sem.at[1], grecv_sem.at[1], ids["y"])
    g_y.start()
    near[1].second()
    near[2].start()
    wide[0].start()
    stores = [
        pltpu.make_async_copy(own_f, wf_out.at[:, own_rows, :], store_sem.at[0]),
        pltpu.make_async_copy(own_d, wd_out.at[:, pl.ds(pl.multiple_of(fs * (FF // 16), 16), FF // 16), :], store_sem.at[1]),
    ]
    for c in stores:
        c.start()
    ends = seq_ends(len_ref)
    token = lax.broadcasted_iota(jnp.int32, (1, count), 1)
    start = jnp.zeros((1, count), jnp.int32)
    for e in ends:
        start = jnp.where(token >= e, e, start)
    angle = freq_ref[:, 0:1] * (token - start).astype(f32)
    cosine, sine = jnp.cos(angle), jnp.sin(angle)
    cos_s[...] = jnp.concatenate([cosine] * 4, axis=0).T
    sin_s[...] = jnp.concatenate([-sine, sine, -sine, sine], axis=0).T
    near[2].second()
    wide[1].start()
    proj.start()
    near[1].third()
    g_y.wait()
    gain_out[...] = gain_c[0] + gain_c[1]
    g1 = gain_out[0:1, :]
    load_x.wait()

    @pl.loop(0, count // BLK)
    def _(i):
        blk = pl.ds(pl.multiple_of(i * BLK, BLK), BLK)
        x = x_s[blk, :].astype(f32)
        inverse = lax.rsqrt(jnp.mean(x * x, axis=-1, keepdims=True) + norm_eps)
        h1_s[blk, :] = (x * inverse * g1).astype(bf16)

    near[0].second()
    wide[0].second()
    wide[2].start()
    near[2].third()
    fill_bias(ends, bias, count)
    near[1].fourth()
    wide[3].start()

    def project(c):
        h1 = h1_s[...]
        for t in range(3):
            block = dot(h1, joined(wq_s, 6 * c + 2 * t, 2), 1, 0)
            for i in range(2):
                p = 2 * c + i
                piece = block[:, 128 * i:128 * i + 128]
                if t == 0:
                    q_s[p] = (rope(piece, cos_s[...], sin_s[...], 1) * (LOG2E / 8)).astype(bf16)
                elif t == 1:
                    k_s[p] = rope(piece, cos_s[...], sin_s[...], 1).astype(bf16)
                else:
                    v_s[p] = piece.astype(bf16)
                    vt_s[p] = piece.T.astype(bf16)

    def scores(p, i, h):
        q = q_s[p, i * BLK:(i + 1) * BLK, :]
        return dot(k_s[p, :BLK * (i + 1), :], jnp.where(lane_head(h, q.shape), q, 0), 1, 1)

    def soft(p, i, h, s):
        s = s + bias[:BLK * (i + 1), i * BLK:(i + 1) * BLK]
        largest = jnp.max(s, axis=0, keepdims=True)
        e = jnp.exp2(s - largest)
        total = jnp.sum(e, axis=0, keepdims=True)
        log_s[p, h:h + 1, i * BLK:(i + 1) * BLK] = largest + jnp.log2(total)
        return e.astype(bf16), total

    def mix(p, i, h, e, total):
        return dot(vt_s[p, 64 * h:64 * h + 64, :BLK * (i + 1)], e, 1, 0) * (1.0 / total)

    def attend(p):
        tasks = [(i, h) for i in range(count // BLK) for h in range(2)]
        s = scores(p, *tasks[0])
        held = None
        outs = {}
        for n, task in enumerate(tasks):
            ahead = scores(p, *tasks[n + 1]) if n + 1 < len(tasks) else None
            weighted = soft(p, *task, s)
            if held is not None:
                outs[held[0]] = mix(p, *held[0], *held[1])
            held = (task, weighted)
            s = ahead
        outs[held[0]] = mix(p, *held[0], *held[1])
        cols = pl.ds(pl.multiple_of(p * 128, 128), 128)
        for i in range(count // BLK):
            both = jnp.concatenate([outs[i, 0], outs[i, 1]], axis=0)
            at_s[cols, i * BLK:(i + 1) * BLK] = both.astype(bf16)
            a_s[i * BLK:(i + 1) * BLK, cols] = both.T.astype(bf16)

    ready = [pltpu.make_async_copy(src, dst, store_sem.at[3 + i]) for i, (src, dst) in enumerate((
        (wq_s, wq_out), (q_s, q_out), (k_s, k_out), (v_s, v_out), (cos_s, cos_out), (sin_s, sin_out)))]
    arrivals = [[near[0].arrive], [near[1].arrive], [near[2].arrive]]
    projected = [
        [near[2].fourth, wide[1].second, wide[0].third, down.start],
        [down.second, proj.third],
        [c.start for c in ready],
    ]
    attended = [
        [wide[1].third, wide[2].second, proj.second],
        [wide[0].fourth, wide[3].second, wide[2].third],
        [wide[1].fourth, wide[3].third],
        [wide[2].fourth, down.third, proj.fourth],
        [wide[3].fourth],
        [down.fourth],
    ]

    def at_turn(c, lists):
        for turn, steps in enumerate(lists):
            if steps:
                @pl.when(c == turn)
                def _():
                    for step in steps:
                        step()

    @pl.loop(0, 3)
    def _(c):
        at_turn(c, arrivals)
        project(c)
        at_turn(c, projected)

        @pl.loop(2 * c, 2 * c + 2)
        def _(p):
            attend(p)
            at_turn(p, attended)
    stores += ready
    proj.arrive()
    for i, (src, dst) in enumerate(((wo_s, wo_out), (a_s, a_out), (at_s, at_out), (log_s, log_out))):
        c = pltpu.make_async_copy(src, dst, store_sem.at[10 + i])
        c.start()
        stores.append(c)

    @pl.loop(0, count // BLK)
    def _(i):
        blk = pl.ds(pl.multiple_of(i * BLK, BLK), BLK)
        mid_s[blk, :] = x_s[blk, :].astype(f32) + dot(a_s[blk, :], joined(wo_s, 0, 6), 1, 0)
    c = pltpu.make_async_copy(mid_s, mid_out, store_sem.at[14])
    c.start()
    stores.append(c)

    @pl.loop(0, count // BLK)
    def _(i):
        blk = pl.ds(pl.multiple_of(i * BLK, BLK), BLK)
        h1t_s[:, blk] = h1_s[blk, :].astype(f32).T.astype(bf16)
    c = pltpu.make_async_copy(h1t_s, h1t_out, store_sem.at[9])
    c.start()
    stores.append(c)
    for g in wide + [down]:
        g.arrive()
    for g in near + [proj] + wide + [down]:
        g.sent()
    for c in stores:
        c.wait()


def frequencies():
    half = 32
    frequency = rope_base ** (-2.0 * np.arange(half) / (2 * half))
    return jnp.asarray(np.broadcast_to(frequency[:, None], (half, 128)), f32)


def forward(reps, lengths, tokens, gains, w_qkv, w_proj, w_ffn, w_down):
    count, width = tokens.shape
    pairs = width // 128
    S = jax.ShapeDtypeStruct
    V = pltpu.VMEM
    rows = width // 4
    dma = pltpu.SemaphoreType.DMA
    return pl.pallas_call(
        functools.partial(forward_kernel, reps),
        name="gather_forward",
        in_specs=[SM, ANY, VM, VM, ANY, ANY, ANY, ANY],
        out_specs=[ANY] * 12 + [VM] + [ANY] * 2,
        out_shape=[S((18, width, 128), bf16), S((6, width, 128), bf16), S((32, width, 128), bf16), S((4, FF // 4, width), bf16),
                   S((pairs, count, 128), bf16), S((pairs, count, 128), bf16), S((pairs, count, 128), bf16),
                   S((count, width), bf16), S((width, count), bf16), S((width, count), bf16), S((pairs, 8, count), f32),
                   S((count, width), f32), S((8, width), f32),
                   S((count, 128), f32), S((count, 128), f32)],
        scratch_shapes=[
            V((18, width, 128), bf16), V((6, width, 128), bf16), V((rows, 3 * width), f32), V((rows, width), f32),
            V((rows, 2 * FF), f32), V((FF // 4, width), f32), V((32, rows, 128), bf16), V((4, FF // 16, width), bf16),
            V((8, width), f32), V((8, width), f32), V((2, 8, width), f32),
            V((count, width), bf16), V((count, 128), f32), V((count, 128), f32),
            V((count, width), bf16), V((width, count), bf16), V((pairs, count, 128), bf16), V((pairs, count, 128), bf16),
            V((pairs, 128, count), bf16), V((pairs, count, 128), bf16), V((count, width), bf16), V((width, count), bf16),
            V((pairs, 8, count), f32), V((count, width), f32), V((count, count), f32),
            dma((5,)), dma((15,)), dma((9, 13)), dma((9, 13)), dma((2,)), dma((2,))],
        compiler_params=pltpu.CompilerParams(collective_id=0, has_side_effects=True, vmem_limit_bytes=60 * 2**20),
    )(lengths, tokens, gains, frequencies(), w_qkv, w_proj, w_ffn, w_down)


class Reduce:
    def __init__(self, ids, reps, grad, slots, kept, out, sems, out_sem):
        self.ids = ids
        self.grad, self.slots, self.kept, self.out = grad, slots, kept, out
        self.ssem, self.rsem = sems
        self.out_sem = out_sem
        rep, fs = ids["rep"], ids["fsdp"]
        self.core, self.y = fs % 2, fs // 2
        self.half = rep % 2
        self.z = 2 * (rep // 2 % 2) + rep // 4 % 2
        self.extra = reps.bit_length() - 1 - 3
        self.stages = 7 + self.extra
        self.offsets = stage_offsets(reps)
        self.lags = stage_lags(reps)

    def cp(self, kind, par, src, dst, device):
        return remote(src, dst, self.ssem.at[kind, par], self.rsem.at[kind, par], self.ids[device])

    def exchange(self, k, n):
        g = self.grad.at[n % SLOTS]
        mine = g.at[self.core, self.y]
        keep = self.kept.at[n]
        par = n % (2 * self.lags[k])
        first = 4 * self.half
        own = keep.at[pl.ds(first + self.z, 1)]
        if k == 0:
            return [self.cp(0, par, g.at[1 - self.core], self.slots[0].at[par], "core")]
        if k == 1:
            return [self.cp(1, par, g.at[self.core, 1 - self.y], self.slots[1].at[par], "y")]
        if k == 2:
            return [self.cp(2, par, mine.at[pl.ds(4 - first, 4)], self.slots[2].at[par], "bit0")]
        if k == 3:
            return [self.cp(2 + d, par, mine.at[first + (self.z ^ d)], self.slots[3].at[par, d - 1], "z%d" % d) for d in (1, 2, 3)]
        if k < 4 + self.extra:
            return [self.cp(6 + k, par, own, self.slots[k].at[par], "bit%d" % (k - 1))]
        if k == 4 + self.extra:
            return [self.cp(5 + d, par, own, own, "z%d" % d) for d in (1, 2, 3)]
        part = keep.at[pl.ds(first, 4)]
        return [self.cp(9, par, part, part, "bit0")]

    def start(self, k, n):
        for c in self.exchange(k, n):
            c.start()

    def add(self, n, first, number, slot, offset):
        mine = self.grad.at[n % SLOTS, self.core, self.y]

        @pl.loop(0, number)
        def _(i):
            mine[first + i] = (mine[first + i].astype(f32) + slot[offset + i].astype(f32)).astype(bf16)

    def stage(self, k, n):
        par = n % (2 * self.lags[k - 1])
        first = 4 * self.half
        if k > 0:
            for c in self.exchange(k - 1, n):
                c.wait()
        if k == 0:
            self.start(0, n)
        elif k == 1:
            g, slot = self.grad.at[n % SLOTS, self.core], self.slots[0].at[par]
            for y in (1 - self.y, self.y):
                @pl.loop(0, 8)
                def _(i):
                    g[y, i] = (g[y, i].astype(f32) + slot[y, i].astype(f32)).astype(bf16)
                if y is not self.y:
                    self.start(1, n)
        elif k == 2:
            self.add(n, 4 - first, 4, self.slots[1].at[par], 4 - first)
            self.start(2, n)
            self.add(n, first, 4, self.slots[1].at[par], first)
        elif k == 3:
            self.add(n, first, 4, self.slots[2].at[par], 0)
            self.start(3, n)
        elif k == 4:
            own = first + self.z
            slot = self.slots[3].at[par]
            total = self.grad[n % SLOTS, self.core, self.y, own].astype(f32) + slot[0].astype(f32)
            self.kept[n, own] = (total + slot[1].astype(f32) + slot[2].astype(f32)).astype(bf16)
            self.start(4, n)
        elif k <= 4 + self.extra:
            own = first + self.z
            slot = self.slots[k - 1].at[par]
            self.kept[n, own] = (self.kept[n, own].astype(f32) + slot[0].astype(f32)).astype(bf16)
            self.start(k, n)
        elif k < self.stages - 1:
            self.start(k, n)
        else:
            self.store(n).start()

    def store(self, n):
        return pltpu.make_async_copy(self.kept.at[n], self.out.at[n], self.out_sem.at[n])

    def tick(self, time):
        for k in reversed(range(self.stages)):
            since = time - self.offsets[k]
            if isinstance(time, int):
                if since < 0 or (since > 8 and since % 2) or since > 2 * CHUNKS - 10:
                    continue
                self.stage(k, since if since <= 8 else (since + 8) // 2)
            else:
                late = (since + 8) // 2
                fits = jnp.logical_and(since >= 0, jnp.logical_or(since <= 8, jnp.logical_and(since == 2 * late - 8, late < CHUNKS)))

                @pl.when(fits)
                def _():
                    self.stage(k, jnp.where(since <= 8, since, late))

    def last_tick(self):
        return 2 * CHUNKS - 10 + self.offsets[-1]


def stage_offsets(reps):
    stages = 7 + reps.bit_length() - 1 - 3
    return [0] + [1 + sum(LAGS[i] if i < len(LAGS) else LAGS[-1] for i in range(k)) for k in range(stages - 1)]


def stage_lags(reps):
    offsets = stage_offsets(reps)
    return [b - a for a, b in zip(offsets, offsets[1:])]


def put_pieces(slot, value, block):
    for s in range(4):
        for i in range(2):
            half, c = divmod(block + i, 3)
            for r in range(4):
                row = 192 * s + 48 * r
                slot[s % 2, s // 2, r + 4 * half, 48 * c:48 * c + 48, :] = value[row:row + 48, 128 * i:128 * i + 128]


def backward_kernel(reps, len_ref, gain_ref, x_in, cot_in, mid_in, q_in, k_in, v_in, a_in, at_in, h1t_in, log_in, cos_in, sin_in,
                    wq_in, wo_in, wf_in, wd_in,
                    block_out, input_grad, grad_out, gain_out,
                    mid_s, dmid_s, dy_s, x_s, cos_s, sin_s, wq_s, wo_s, out_s,
                    grad_s, kept_s, gain_s, send_sem, recv_sem, gsend_sem, grecv_sem, out_sem, load_sem, store_sem, *slots):
    count, width = x_s.shape
    rows = width // 4
    blocks = count // BLK
    rep, fs = lax.axis_index("rep"), lax.axis_index("fsdp")
    ids = partners(rep, fs, reps)
    bits = reps.bit_length() - 1
    names = ("core", "y") + tuple("bit%d" % b for b in range(bits))
    friends = names[:3] + ("z1", "z2", "z3") + names[5:]
    red = Reduce(ids, reps, grad_s, slots, kept_s, grad_out, (send_sem, recv_sem), out_sem)
    ends = seq_ends(len_ref)
    valid = ends[3]

    def load(i, src, dst):
        c = pltpu.make_async_copy(src, dst, load_sem.at[i])
        c.start()
        return c

    g1, g2 = gain_ref[0:1, :], gain_ref[1:2, :]

    def feed(wf_s, wd_s, h2_s, h2t_s, z_s, df_s):
        greet(ids, friends)
        need = [load(0, mid_in, mid_s), load(1, cot_in, dy_s)]
        def weights(j):
            return [pltpu.make_async_copy(wf_in.at[pl.ds(8 * j, 8)], wf_s.at[pl.ds(8 * j, 8)], load_sem.at[2 + 2 * j]),
                    pltpu.make_async_copy(wd_in.at[j], wd_s.at[j], load_sem.at[3 + 2 * j])]

        for j in range(4):
            for c in weights(j):
                c.start()
        late = [load(10, x_in, x_s), load(11, cos_in, cos_s), load(12, sin_in, sin_s), load(13, wq_in, wq_s),
                load(14, wo_in, wo_s)]
        for c in need:
            c.wait()

        @pl.loop(0, blocks)
        def _(i):
            blk = rows_of(i)
            unit, _ = unit_rows(mid_s[blk, :])
            h2 = unit * g2
            h2_s[blk, :] = h2.astype(bf16)
            h2t_s[:, blk] = h2.T.astype(bf16)
            token = lax.broadcasted_iota(jnp.int32, (BLK, 1), 0) + i * BLK
            dy_s[blk, :] = jnp.where(token < valid, dy_s[blk, :], 0)
            out_s[blk, :] = mid_s[blk, :]
            dmid_s[blk, :] = jnp.zeros((BLK, width), f32)

        meet(friends)

        @pl.loop(0, 4)
        def _(j):
            for c in weights(j):
                c.wait()

            @pl.loop(0, blocks)
            def _(i):
                blk = rows_of(i)
                h2 = h2_s[blk, :]
                gate = dot(h2, joined(wf_s, 8 * j, 4), 1, 0)
                up = dot(h2, joined(wf_s, 8 * j + 4, 4), 1, 0)
                dz = dot(dy_s[blk, :], wd_s[j], 1, 1)
                sg = 1.0 / (1.0 + jnp.exp(-gate))
                silu = gate * sg
                z = (silu * up).astype(bf16)
                z_s[blk, :] = z
                dgate = (dz * up * (sg * (1.0 + gate * (1.0 - sg)))).astype(bf16)
                dup = (dz * silu).astype(bf16)
                df_s[blk, 0:512] = dgate
                df_s[blk, 512:1024] = dup
                out_s[blk, :] += dot(z, wd_s[j], 1, 0)
                dmid_s[blk, :] += dot(jnp.concatenate([dgate, dup], axis=1), joined(wf_s, 8 * j, 8), 1, 1)

            red.tick(2 * j - 1)
            gwd = dot(z_s[...], dy_s[...], 0, 0).astype(bf16)
            for s in range(4):
                for k in range(8):
                    for c in range(6):
                        row = 128 * s + 16 * k
                        grad_s[2 * j, s % 2, s // 2, k, 16 * c:16 * c + 16, :] = gwd[row:row + 16, 128 * c:128 * c + 128]

            @pl.loop(0, 4)
            def _(n):
                gwf = dot(h2t_s[...], df_s[:, pl.ds(pl.multiple_of(256 * n, 256), 256)], 1, 0).astype(bf16)
                for s in range(4):
                    for i in range(2):
                        lanes = slice(128 * i, 128 * i + 128)
                        grad_s[2 * j, s % 2, s // 2, 2 * n + i, 96:144, :] = gwf[rows * s:rows * s + 48, lanes]
                        grad_s[2 * j + 1, s % 2, s // 2, 2 * n + i, 0:144, :] = gwf[rows * s + 48:rows * s + rows, lanes]
            red.tick(2 * j)
        for c in late:
            c.wait()

    V = pltpu.VMEM
    pl.run_scoped(feed, V((32, width, 128), bf16), V((4, FF // 4, width), bf16), V((count, width), bf16),
                  V((width, count), bf16), V((count, 512), bf16), V((count, 1024), bf16))

    def attention(q_s, k_s, v_s, kt_s, a_s, at_s, da_s, log_s, dmb_s, dq3_s, h1t_s, bias, dqt_s):
        need = [load(0, q_in, q_s), load(1, k_in, k_s), load(2, v_in, v_s), load(3, log_in, log_s), load(4, a_in, a_s),
                load(5, at_in, at_s), load(6, h1t_in, h1t_s)]

        gain_s[...] = jnp.zeros_like(gain_s)
        @pl.loop(0, blocks)
        def _(i):
            blk = rows_of(i)
            unit, inverse = unit_rows(mid_s[blk, :])
            dh = dmid_s[blk, :]
            gain_s[0, 1:2, :] += jnp.sum(dh * unit, axis=0, keepdims=True)
            scaled = dh * g2
            dmid = dy_s[blk, :].astype(f32) + inverse * (scaled - unit * jnp.mean(scaled * unit, axis=-1, keepdims=True))
            dmid_s[blk, :] = dmid
            dmb_s[blk, :] = dmid.astype(bf16)
            mid_s[blk, :] = out_s[blk, :]
        red.tick(7)

        @pl.loop(0, 3)
        def _(c):
            part = pl.ds(pl.multiple_of(c * 256, 256), 256)
            weight = jnp.concatenate([wo_s[i, part, :] for i in range(6)], axis=1)
            da = dot(dmb_s[...], weight, 1, 1).astype(bf16)
            da_s[2 * c] = da[:, 0:128]
            da_s[2 * c + 1] = da[:, 128:256]
        need[5].wait()
        for n in range(3):
            gwo = dot(at_s[...], dmb_s[:, 256 * n:256 * n + 256], 1, 0).astype(bf16)
            put_pieces(grad_s.at[8], gwo, 2 * n)
        red.tick(8)
        fill_bias(ends, bias, count)
        for c in need[:5] + need[6:]:
            c.wait()

        def pair(p, place):
            kt_s[...] = k_s[p].T
            cols = pl.ds(pl.multiple_of(p * 128, 128), 128)
            product = da_s[p].astype(f32) * a_s[:, cols].astype(f32)
            pick = ((lax.broadcasted_iota(jnp.int32, (8, 128), 1) // 64)
                    == lax.broadcasted_iota(jnp.int32, (8, 128), 0)).astype(bf16)
            high = product.astype(bf16)
            low = (product - high.astype(f32)).astype(bf16)
            centred = dot(pick, high, 1, 1) + dot(pick, low, 1, 1)

            def first(j, h):
                lo = j * BLK
                q, da = q_s[p, lo:, :], da_s[p, lo:, :]
                mine = lane_head(h, q.shape)
                q, da = jnp.where(mine, q, 0), jnp.where(mine, da, 0)
                return dot(k_s[p, lo:lo + BLK, :], q, 1, 1), dot(v_s[p, lo:lo + BLK, :], da, 1, 1), q, da

            def middle(j, h, s, dp):
                lo = j * BLK
                weight = jnp.exp2(s + bias[lo:lo + BLK, lo:] - log_s[p, h:h + 1, lo:])
                ds = (weight * (dp - centred[h:h + 1, lo:])).astype(bf16)
                return weight.astype(bf16), ds

            sums = {}

            def last(j, h, weight, ds, q, da):
                lo = j * BLK
                dv, dk = dot(weight, da, 1, 0), dot(ds, q, 1, 0)
                dq = dot(kt_s[64 * h:64 * h + 64, lo:lo + BLK], ds, 1, 0)
                if j == 0:
                    dqt_s[64 * h:64 * h + 64, :] = dq
                else:
                    dqt_s[64 * h:64 * h + 64, lo:] += dq
                if j in sums:
                    dk, dv = dk + sums[j][0], dv + sums[j][1]
                    dk = rope(dk * (1.0 / LOG2E), cos_s[lo:lo + BLK, :], sin_s[lo:lo + BLK, :], -1)
                    dq3_s[place + 2, lo:lo + BLK, :] = dk.astype(bf16)
                    dq3_s[place + 4, lo:lo + BLK, :] = dv.astype(bf16)
                else:
                    sums[j] = (dk, dv)

            tasks = [(j, h) for j in range(blocks) for h in range(2)]
            now = first(*tasks[0])
            held = None
            for n, task in enumerate(tasks):
                ahead = first(*tasks[n + 1]) if n + 1 < len(tasks) else None
                pd = middle(*task, now[0], now[1])
                if held is not None:
                    last(*held)
                held = (*task, *pd, now[2], now[3])
                now = ahead
            last(*held)
            dq3_s[place] = rope(dqt_s[...].T * 0.125, cos_s[...], sin_s[...], -1).astype(bf16)

        @pl.loop(0, 3)
        def _(c):
            @pl.loop(0, 2)
            def _(i):
                pair(2 * c + i, 6 * c + i)

                @pl.when(i == 0)
                def _():
                    red.tick(9 + 2 * c)
            for t in range(3):
                gwq = dot(h1t_s[...], joined(dq3_s, 6 * c + 2 * t, 2), 1, 0).astype(bf16)
                put_pieces(grad_s.at[c], gwq, 2 * t)
            red.tick(10 + 2 * c)

        @pl.loop(0, blocks)
        def _(i):
            blk = rows_of(i)
            dq3 = jnp.concatenate([dq3_s[n, blk, :] for n in range(18)], axis=1)
            dh = dot(dq3, joined(wq_s, 0, 18), 1, 1)
            unit, inverse = unit_rows(x_s[blk, :].astype(f32))
            gain_s[0, 0:1, :] += jnp.sum(dh * unit, axis=0, keepdims=True)
            scaled = dh * g1
            dmid_s[blk, :] += inverse * (scaled - unit * jnp.mean(scaled * unit, axis=-1, keepdims=True))
            dmb_s[blk, :] = mid_s[blk, :].astype(bf16)
            red.tick(15 + i)

        a = pltpu.make_async_copy(dmid_s, input_grad, store_sem.at[0])
        b = pltpu.make_async_copy(dmb_s, block_out, store_sem.at[1])
        a.start()
        b.start()
        step = 0
        pending = None
        drain = 15 + blocks
        while drain + step <= red.last_tick() or step <= len(names):
            if pending is not None:
                pending.wait()
                gain_s[step] = gain_s[step - 1] + gain_s[len(names) + step]
                pending = None
            if step < len(names):
                pending = remote(gain_s.at[step], gain_s.at[len(names) + 1 + step], gsend_sem.at[step], grecv_sem.at[step],
                                 ids[names[step]])
                pending.start()
            red.tick(drain + step)
            step += 1
        gain_out[...] = pltpu.roll(gain_s[len(names)], width - fs * rows, 1)
        a.wait()
        b.wait()

    pairs = width // 128
    pl.run_scoped(attention, V((pairs, count, 128), bf16), V((pairs, count, 128), bf16), V((pairs, count, 128), bf16),
                  V((128, count), bf16), V((count, width), bf16), V((width, count), bf16), V((pairs, count, 128), bf16),
                  V((pairs, 8, count), f32),
                  V((count, width), bf16), V((18, count, 128), bf16), V((width, count), bf16), V((count, count), f32),
                  V((128, count), f32))
    for n in range(CHUNKS):
        red.store(n).wait()


def backward(reps, lengths, gain, tokens, cotangent, mid, q, k, v, a, at, h1t, log, cosine, sine, wq, wo, wf, wd):
    count, width = tokens.shape
    S = jax.ShapeDtypeStruct
    V = pltpu.VMEM
    dma = pltpu.SemaphoreType.DMA
    bits = reps.bit_length() - 1
    steps = 2 + bits
    exchanges = 10 + bits - 3
    lags = stage_lags(reps)
    shapes = [(2, 8), (8,), (4,), (3,)] + [(1,)] * (bits - 3)
    slots = [V((2 * lags[k],) + shape + (PIECE, 128), bf16) for k, shape in enumerate(shapes)]
    return pl.pallas_call(
        functools.partial(backward_kernel, reps),
        name="backward_reduce",
        in_specs=[SM, VM] + [ANY] * 16,
        out_specs=[ANY] * 3 + [VM],
        out_shape=[S((count, width), bf16), S((count, width), f32), S((CHUNKS, 8, PIECE, 128), bf16), S((8, width), f32)],
        scratch_shapes=[
            V((count, width), f32), V((count, width), f32), V((count, width), bf16), V((count, width), bf16),
            V((count, 128), f32), V((count, 128), f32), V((18, width, 128), bf16), V((6, width, 128), bf16),
            V((count, width), f32),
            V((SLOTS, 2, 2, 8, PIECE, 128), bf16), V((CHUNKS, 8, PIECE, 128), bf16), V((2 * steps + 1, 8, width), f32),
            dma((exchanges, 2 * max(lags))), dma((exchanges, 2 * max(lags))), dma((steps,)), dma((steps,)), dma((CHUNKS,)), dma((15,)), dma((2,))] + slots,
        compiler_params=pltpu.CompilerParams(collective_id=1, has_side_effects=True, vmem_limit_bytes=62 * 2**20),
    )(lengths, gain, tokens, cotangent, mid, q, k, v, a, at, h1t, log, cosine, sine, wq, wo, wf, wd)


def adamw(weight, first, second, grad, rate):
    first_new = beta_first * first + (1.0 - beta_first) * grad
    second_new = beta_second * second + (1.0 - beta_second) * grad * grad
    first_hat = first_new * (1.0 / (1.0 - beta_first**STEP))
    second_hat = second_new * (1.0 / (1.0 - beta_second**STEP))
    return (
        first_new,
        second_new,
        weight - rate * (first_hat / (jnp.sqrt(second_hat) + adam_eps) + decay_rate * weight),
    )


def update_tasks(width):
    rows = width // 4
    tasks = []
    for t in range(3):
        cols = [[(9 + c, r + 4 * ((2 * t + i) // 3), 48 * ((2 * t + i) % 3), 48) for r in range(4)]
                for c in range(3) for i in range(2)]
        tasks.append((0, (0, rows), t * width, cols))
    for k in range(8):
        tasks.append((2, (0, rows), 512 * k, [[(2 * j, k, 96, 48), (2 * j + 1, k, 0, 144)] for j in range(4)]))
    for j in range(4):
        tasks.append((3, (128 * j, 128), 0, [[(2 * j, k, 16 * c, 16) for k in range(8)] for c in range(6)]))
    tasks.append((1, (0, rows), 0, [[(8, r + 4 * (b // 3), 48 * (b % 3), 48) for r in range(4)] for b in range(6)]))
    return tasks


def update_kernel(rates, tasks, depth, grad_ref, gain_grad, *refs):
    passed, refs = refs[:2], refs[2:]
    state, refs = refs[:12], refs[12:]
    gain_state, refs = refs[:3], refs[3:]
    new, refs = refs[:12], refs[12:]
    gain_new, refs = refs[:3], refs[3:]
    given, refs = refs[:2], refs[2:]
    taken, made, in_sem, out_sem, low_s, wide_s, pass_sem = refs
    holds = (low_s, wide_s)
    through = [pltpu.make_async_copy(passed[i], holds[i], pass_sem.at[i]) for i in range(2)]
    onward = [pltpu.make_async_copy(holds[i], given[i], pass_sem.at[2 + i]) for i in range(2)]

    def moves(n, out):
        w, (row, rows), col, cols = tasks[n]
        wide = 128 * len(cols)
        slot = n % depth
        found = []
        for i in range(3):
            if out:
                found.append(pltpu.make_async_copy(made.at[slot, i, pl.ds(0, rows), pl.ds(0, wide)],
                                                   new[3 * w + i].at[pl.ds(row, rows), pl.ds(col, wide)], out_sem.at[slot, i]))
            else:
                found.append(pltpu.make_async_copy(state[3 * w + i].at[pl.ds(row, rows), pl.ds(col, wide)],
                                                   taken.at[slot, i, pl.ds(0, rows), pl.ds(0, wide)], in_sem.at[slot, i]))
        return found

    for n in range(depth):
        for c in moves(n, False):
            c.start()
    columns = gain_grad[0:2, 0:gain_new[0].shape[1]]
    for ref, value in zip((gain_new[1], gain_new[2], gain_new[0]), adamw(gain_state[0][...], gain_state[1][...], gain_state[2][...], columns, 1.0)):
        ref[...] = value
    for n, (w, (_, rows), _, cols) in enumerate(tasks):
        slot = n % depth
        for c in moves(n, False):
            c.wait()
        if n >= depth:
            for c in moves(n - depth, True):
                c.wait()
        for i, pieces in enumerate(cols):
            grad = jnp.concatenate([grad_ref[c, p, r:r + m, :] for c, p, r, m in pieces], axis=0).astype(f32)
            lanes = slice(128 * i, 128 * i + 128)
            held = [taken[slot, s, 0:rows, lanes] for s in range(3)]
            for s, value in zip((1, 2, 0), adamw(held[0], held[1], held[2], grad, rates[w])):
                made[slot, s, 0:rows, lanes] = value
        for c in moves(n, True):
            c.start()
        if n + depth < len(tasks):
            for c in moves(n + depth, False):
                c.start()
        if n == 2:
            for c in through:
                c.start()
        if n == 8:
            for a, b in zip(through, onward):
                a.wait()
                b.start()
    for n in range(len(tasks) - depth, len(tasks)):
        for c in moves(n, True):
            c.wait()
    for c in onward:
        c.wait()


def update(rates, grads, gain_grad, through, state, gain_state):
    width = gain_grad.shape[1]
    S = jax.ShapeDtypeStruct
    depth = 6
    dma = pltpu.SemaphoreType.DMA
    return pl.pallas_call(
        functools.partial(update_kernel, rates, update_tasks(width), depth),
        name="update",
        in_specs=[VM, VM] + [ANY] * 14 + [VM] * 3,
        out_specs=[ANY] * 12 + [VM] * 3 + [ANY] * 2,
        out_shape=[S(z.shape, z.dtype) for z in state + gain_state + through],
        scratch_shapes=[pltpu.VMEM((depth, 3, width // 4, width), f32), pltpu.VMEM((depth, 3, width // 4, width), f32),
                        dma((depth, 3)), dma((depth, 3))]
        + [pltpu.VMEM(z.shape, z.dtype) for z in through] + [dma((4,))],
        compiler_params=pltpu.CompilerParams(vmem_limit_bytes=60 * 2**20),
    )(grads, gain_grad, *through, *state, *gain_state)


def shards(reps, tokens, cotangent, lengths, w_qkv, m_qkv, v_qkv, w_proj, m_proj, v_proj, w_ffn, m_ffn, v_ffn,
           w_down, m_down, v_down, gains, m_gains, v_gains):
    count, width = tokens.shape
    wq, wo, wf, wd, q, k, v, a, at, h1t, log, mid, gain, cosine, sine = forward(
        reps, lengths, tokens, gains, w_qkv, w_proj, w_ffn, w_down)
    block_out, input_grad, grads, gain_grad = backward(
        reps, lengths, gain, tokens, cotangent, mid, q, k, v, a, at, h1t, log, cosine, sine, wq, wo, wf, wd)
    wide = 3.0 * width ** (-0.5)
    proj = 3.0 * (count / (10.0 * width)) ** 0.5
    down = 6.0 * FF ** (-0.5)
    new = update(
        (wide, proj, wide, down), grads, gain_grad, (block_out, input_grad),
        (w_qkv, m_qkv, v_qkv, w_proj, m_proj, v_proj, w_ffn, m_ffn, v_ffn, w_down, m_down, v_down),
        (gains, m_gains, v_gains))
    return (new[15], new[16]) + tuple(new[3 * w + s] for w in range(5) for s in (1, 2, 0))


def solution(mesh):
    reps = mesh.shape["rep"]
    tokens = P(("rep", "fsdp"), None)
    weight = P("fsdp", None)
    gain = P(None, "fsdp")
    return jax.shard_map(
        functools.partial(shards, reps),
        mesh=mesh,
        in_specs=(tokens,) * 3 + (weight,) * 12 + (gain,) * 3,
        out_specs=(tokens,) * 2 + (weight,) * 12 + (gain,) * 3,
        check_vma=False,
    )
```
